32 devices in a mesh: gx: 4 (over y, x), gy: 4 (over z), gz: 2 (over core).
Axes of the slice: x: 2, y: 2, z: 4, core: 2. Of those that a mesh axis runs over, the one named last changes fastest.
Arguments:
- dual_rhs: float32 [4, 4, 4, 3, 16, 256], P('gx', 'gy', 'gz'), may hold values from -15 to 15
- factors: bfloat16 [4, 4, 4, 6, 6, 256, 256], P('gx', 'gy', 'gz'), may hold values from -0.1875 to 0.1875
- block_pattern: int32 [4, 4, 4, 6, 6], P('gx', 'gy', 'gz'), may hold values from 0 to 1, as said below
- face_map: int32 [4, 4, 4, 3, 256], P('gx', 'gy', 'gz'), may hold values from 0 to 255, each once within a row
- rigid_modes: float32 [4, 4, 4, 6, 6, 256], P('gx', 'gy', 'gz'), may hold values from -0.21875 to 0.21875
- coarse_solve: float32 [384, 384], P(('gx', 'gy', 'gz')), may hold values from -1 to 2, as said below
Outputs:
- multipliers: float32 [4, 4, 4, 3, 16, 256], P('gx', 'gy', 'gz')
- residual: float32 [4, 4, 4, 3, 16, 256], P('gx', 'gy', 'gz')
The draws below stay inside these ranges and needn't reach their ends.
Inputs may be any that keep to these rules, and one draw needn't show every extreme that they name: `block_pattern`: the diagonal blocks are always present. coarse_solve is symmetric.
All inputs are finite; a program needn't handle non-finite values.
Results may differ from the reference program's by a relative error of at most 0.0019.
Values sent between devices are 32-bit elements; how exact they have to be, the bound alone decides.
No kernel may reach another device: no remote copies, remote signals or barrier semaphores. Data moves between devices by JAX's collectives and lax.ppermute only.
A program may use at most 64 MiB of HBM per device.

```python
import jax
import jax.numpy as jnp
from jax import lax

FD = 256
CASES = 16
MODES = 6
FACES = 6
ITERS = 4
SX = 4
SY = 4
SZ = 4
NC = 384


def draw_dual_rhs(key, part):
    key = jax.random.fold_in(key, 11)
    shape = (SX, SY, SZ, 3, CASES, FD)
    count = SX * SY * SZ
    index = jnp.arange(count, dtype=jnp.float32).reshape(SX, SY, SZ)
    scale = 1.0 + 2.0 * index / max(count - 1, 1)
    scale = scale[:, :, :, None, None, None]
    base = jnp.clip(jax.random.normal(key, shape, jnp.float32), -5.0, 5.0)
    return (base * scale).astype(jnp.float32)


def draw_block_pattern(key, part):
    key = jax.random.fold_in(key, 23)
    shape = (SX, SY, SZ, FACES, FACES)
    random_bits = jax.random.randint(key, shape, 0, 2, jnp.int32)
    diagonal = (jnp.arange(FACES)[:, None] == jnp.arange(FACES)[None, :]).astype(jnp.int32)
    return jnp.maximum(random_bits, diagonal[None, None, None, :, :]).astype(jnp.int32)


def draw_coarse_solve(key, part):
    key = jax.random.fold_in(key, 37)
    raw = jnp.clip(jax.random.normal(key, (NC, NC), jnp.float32), -5.0, 5.0)
    symmetric = (raw + raw.T) * (0.7071 / NC ** 0.5)
    return (symmetric + jnp.eye(NC, dtype=jnp.float32)).astype(jnp.float32)


def shard_levels(own_key, dims, pieces, least, largest):
    loudness = 1.0
    for position, blocks in pieces:
        draws = jax.random.uniform(jax.random.fold_in(jax.random.fold_in(own_key, 6), position), (blocks,), jnp.float32, least / len(pieces), largest / len(pieces))
        loudness = loudness * jnp.repeat(jnp.exp(draws), dims[position] // blocks).reshape((-1,) + (1,) * (len(dims) - 1 - position))
    return loudness


def scatter_about(own_key, shape, deviation, bound, cuts=(), held_as=jnp.bfloat16):
    array = deviation * jax.random.normal(own_key, shape, jnp.float32)
    if cuts:
        array = array * shard_levels(own_key, shape, cuts, -0.22, 0.18)
    return jnp.clip(array, -bound, bound).astype(held_as)


def setup_inputs(seed: int = 0) -> dict:
    streams_of = jax.random.split(jax.random.key(seed), 7)
    dual_rhs = draw_dual_rhs(jax.random.fold_in(streams_of[6], 71), 0)
    factors = scatter_about(streams_of[1], (SX, SY, SZ, FACES, FACES, FD, FD), (4 * FD) ** -0.5, 0.1875, ((0, 4), (1, 4), (2, 2)))
    block_pattern = draw_block_pattern(jax.random.fold_in(streams_of[6], 71), 0)
    face_map = jax.vmap(lambda own: jax.random.permutation(own, FD))(jax.random.split(streams_of[3], SX * SY * SZ * 3)).reshape((SX, SY, SZ, 3, FD)).astype(jnp.int32)
    rigid_modes = scatter_about(streams_of[4], (SX, SY, SZ, FACES, MODES, FD), (4 * FACES * FD // 9) ** -0.5, 0.21875, ((0, 4), (1, 4), (2, 2)), jnp.float32)
    coarse_solve = draw_coarse_solve(jax.random.fold_in(streams_of[6], 71), 0)
    return {"dual_rhs": dual_rhs, "factors": factors, "block_pattern": block_pattern, "face_map": face_map, "rigid_modes": rigid_modes, "coarse_solve": coarse_solve}


highest_prec = lax.Precision.HIGHEST


def lower_take(values, axis_num):
    zeros_part = jnp.zeros_like(lax.slice_in_dim(values, 0, 1, axis=axis_num))
    kept = lax.slice_in_dim(values, 0, values.shape[axis_num] - 1, axis=axis_num)
    return jnp.concatenate([zeros_part, kept], axis=axis_num)


def upper_take(values, axis_num):
    zeros_part = jnp.zeros_like(lax.slice_in_dim(values, 0, 1, axis=axis_num))
    kept = lax.slice_in_dim(values, 1, values.shape[axis_num], axis=axis_num)
    return jnp.concatenate([kept, zeros_part], axis=axis_num)


def permute_faces(values, indices):
    return jnp.take_along_axis(values, jnp.broadcast_to(indices[:, :, :, :, None, :], values.shape), axis=5)


def spread_dual(values, face_map):
    outgoing = permute_faces(values, face_map)
    minus = jnp.stack([lower_take(outgoing[:, :, :, axis_num], axis_num) for axis_num in range(3)], axis=3)
    return jnp.concatenate([values, -minus], axis=3)


def jump_dual(interface, inverse_map, mask):
    minus = interface[:, :, :, 3:]
    above = jnp.stack([upper_take(minus[:, :, :, axis_num], axis_num) for axis_num in range(3)], axis=3)
    return (interface[:, :, :, :3] - permute_faces(above, inverse_map)) * mask


def one_forward(operands):
    weights, blocks, vectors = operands
    products = jnp.einsum('ijab,jcb->ijca', weights.astype(jnp.float32), vectors.astype(jnp.float32))
    return jnp.sum(products * blocks[:, :, None, None], axis=1)


def one_backward(operands):
    weights, blocks, vectors = operands
    products = jnp.einsum('ijab,ica->ijcb', weights.astype(jnp.float32), vectors.astype(jnp.float32))
    return jnp.sum(products * blocks[:, :, None, None], axis=0)


def apply_blocks(function, factors, pattern, vectors):
    flat_w = factors.reshape((-1,) + factors.shape[3:])
    flat_p = pattern.reshape((-1,) + pattern.shape[3:]).astype(jnp.float32)
    flat_v = vectors.reshape((-1,) + vectors.shape[3:])
    result = lax.map(function, (flat_w, flat_p, flat_v))
    return result.reshape(vectors.shape)


def reference(dual_rhs, factors, block_pattern, face_map, rigid_modes, coarse_solve):
    inverse_map = jnp.argsort(face_map, axis=-1).astype(jnp.int32)
    ones_grid = jnp.ones((SX, SY, SZ), jnp.float32)
    mask_x = (jnp.arange(SX) < SX - 1).astype(jnp.float32)[:, None, None] * ones_grid
    mask_y = (jnp.arange(SY) < SY - 1).astype(jnp.float32)[None, :, None] * ones_grid
    mask_z = (jnp.arange(SZ) < SZ - 1).astype(jnp.float32)[None, None, :] * ones_grid
    mask = jnp.stack([mask_x, mask_y, mask_z], axis=3)[:, :, :, :, None, None]

    def project(values):
        interface = spread_dual(values, face_map)
        coarse_rhs = jnp.einsum('xyzfmk,xyzfck->xyzmc', rigid_modes, interface, precision=highest_prec)
        coarse_sol = jnp.dot(coarse_solve, coarse_rhs.reshape(-1, CASES), precision=highest_prec)
        coarse_sol = coarse_sol.reshape(SX, SY, SZ, MODES, CASES)
        lifted = jnp.einsum('xyzfmk,xyzmc->xyzfck', rigid_modes, coarse_sol, precision=highest_prec)
        return values - jump_dual(lifted, inverse_map, mask)

    multipliers = jnp.zeros_like(dual_rhs)
    residual = project(dual_rhs)
    rho_now = jnp.sum(residual * residual)
    rho_old = rho_now
    direction = residual
    for iteration in range(ITERS):
        if iteration == 0:
            direction = residual
        else:
            direction = residual + (rho_now / rho_old) * direction
        interface = spread_dual(direction, face_map).astype(jnp.bfloat16)
        forward = apply_blocks(one_forward, factors, block_pattern, interface)
        curvature = jnp.sum(forward * forward)
        forward_half = forward.astype(jnp.bfloat16)
        backward = apply_blocks(one_backward, factors, block_pattern, forward_half)
        image = project(jump_dual(backward, inverse_map, mask))
        step_len = rho_now / curvature
        multipliers = multipliers + step_len * direction
        residual = residual - step_len * image
        if iteration + 1 < ITERS:
            rho_old = rho_now
            rho_now = jnp.sum(residual * residual)
    return multipliers, residual
```

```python
import functools

import jax
import jax.numpy as jnp
import numpy as np
from jax import lax
from jax.experimental import pallas as pl
from jax.experimental.pallas import tpu as pltpu
from jax.sharding import PartitionSpec as P

ITERS = 4
AXES = ("gx", "gy", "gz")
LANES = 128
SLOT = 8
SLOTS = 12
RHO, FF, FD = SLOTS * SLOT, SLOTS * SLOT + 1, SLOTS * SLOT + 2
NT = (((1,), (1,)), ((), ()))
NN = (((1,), (0,)), ((), ()))
f32 = jnp.float32
bf16 = jnp.bfloat16


def own_slot(s):
    return s


def nbr_slot(s, f):
    if f == 0:
        return 4 + s
    if f == 3:
        return 2 + s
    if f == 1:
        return 8 + s
    if f == 4:
        return 6 + s
    if f == 2:
        return 1 if s == 0 else 11
    return 10 if s == 0 else 0


def slot_table(nx, ny, nz, nc):
    table = np.full((nx * ny * nz, LANES), -1, np.int32)
    sz = 2 * nz
    for x in range(nx):
        for y in range(ny):
            for z in range(nz):
                where = [(x, y, 2 * z), (x, y, 2 * z + 1)]
                where += [(x - 1, y, 2 * z), (x - 1, y, 2 * z + 1), (x + 1, y, 2 * z), (x + 1, y, 2 * z + 1)]
                where += [(x, y - 1, 2 * z), (x, y - 1, 2 * z + 1), (x, y + 1, 2 * z), (x, y + 1, 2 * z + 1)]
                where += [(x, y, 2 * z - 1), (x, y, 2 * z + 2)]
                for slot, (a, b, c) in enumerate(where):
                    if 0 <= a < nx and 0 <= b < ny and 0 <= c < sz:
                        first = ((a * ny + b) * sz + c) * 6
                        table[(x * ny + y) * nz + z, slot * SLOT : slot * SLOT + 6] = first + np.arange(6)
    return table


def split2(x):
    high = x.astype(bf16)
    low = (x - high.astype(f32)).astype(bf16)
    return jnp.concatenate([high, low], 0)


def split3(x):
    high = x.astype(bf16)
    rest = x - high.astype(f32)
    mid = rest.astype(bf16)
    low = (rest - mid.astype(f32)).astype(bf16)
    return jnp.concatenate([high, mid, low], 0)


def fold2(x):
    n = x.shape[0] // 2
    return x[:n] + x[n:]


def fold3(x):
    n = x.shape[0] // 3
    return x[:n] + (x[n : 2 * n] + x[2 * n :])


def mm(a, b, dims):
    return lax.dot_general(a, b, dims, preferred_element_type=f32)


def position(sizes):
    index = [lax.axis_index(a) for a in AXES]
    parity = [lax.rem(i, 2) == 1 for i in index]
    masks = []
    for s in range(2):
        row = []
        for f in range(6):
            d = f % 3
            if d == 2 and (s == 0) == (f == 2):
                row.append(None)
            else:
                inside = (index[d] < sizes[d] - 1) if f < 3 else (index[d] > 0)
                row.append(inside.astype(f32))
        masks.append(row)
    return parity, masks


def masked(value, mask):
    return value if mask is None else value * mask


def pick(cond, a, b):
    return jnp.where(cond, a, b)


def pack_kernel(rhs, modes, fmap, coarse, xa, xb, ya, yb, za, zb):
    parity, _ = position((1, 1, 1))
    slabs = -(-coarse.shape[1] // 256)
    for d, outs in ((0, (xa, xb)), (1, (ya, yb))):
        for s in range(2):
            up, down = modes[s, d], modes[s, d + 3]
            first = pick(parity[d], down, up)
            second = pick(parity[d], up, down)
            for out, piece in zip(outs, (first, second)):
                out[24 * s : 24 * s + 16, :] = rhs[s, d]
                out[24 * s + 16 : 24 * s + 24, :] = jnp.concatenate(
                    [piece, fmap[s, d : d + 1, :].astype(f32), jnp.zeros((1, 256), f32)], 0
                )
    up, down = modes[1, 2], modes[0, 5]
    for out, piece in zip((za, zb), (pick(parity[2], down, up), pick(parity[2], up, down))):
        out[0:16, :] = rhs[1, 2]
        out[16:24, :] = jnp.concatenate([piece, fmap[1, 2:3, :].astype(f32), jnp.zeros((1, 256), f32)], 0)
    for k in range(slabs):
        width = min(256, coarse.shape[1] - 256 * k)
        slab = coarse[:, 256 * k : 256 * k + width]
        if width < 256:
            slab = jnp.concatenate([slab, jnp.zeros((12, 256 - width), f32)], 1)
        gap = jnp.zeros((2, 256), f32)
        slab = jnp.concatenate([slab[:6], gap, slab[6:], gap], 0)
        for out, base in ((xa, 48), (xb, 48), (ya, 48), (yb, 48), (za, 24), (zb, 24)):
            out[base + 16 * k : base + 16 * k + 16, :] = slab


def setup_kernel(rhs, modes, fmap, coarse, table, xa, xb, ya, yb, za, zb, perm, lift, start, solve, send, work, rows):
    parity, _ = position((1, 1, 1))
    slabs = -(-coarse.shape[1] // 256)
    devices = table.shape[0]
    lane_row = lax.broadcasted_iota(jnp.int32, (256, 256), 0)

    plus, minus = [], []
    for d, (a, b) in enumerate(((xa, xb), (ya, yb), (za, zb))):
        va, vb = a[...], b[...]
        plus.append(pick(parity[d], vb, va))
        minus.append(pick(parity[d], va, vb))

    def onehot(row):
        return (lane_row == row.astype(jnp.int32)).astype(bf16)

    def to_upper_order(values, table_rows):
        return -fold3(mm(split3(values), table_rows, NT))

    zero2 = jnp.zeros((2, 256), f32)
    partial = [jnp.zeros((48, 256), f32) for _ in range(2)]
    up_perm = {}
    for s in range(2):
        for d in range(3):
            up_perm[s, d] = onehot(fmap[s, d : d + 1, :])
    tilde_low = {}
    for s in range(2):
        for d in range(3):
            if d == 2 and s == 1:
                table_rows = up_perm[0, 2]
            else:
                base = 24 * s if d < 2 else 0
                table_rows = onehot(minus[d][base + 22 : base + 23, :])
            perm[s * 3 + d] = table_rows
            tilde_low[s, d] = to_upper_order(modes[s, d + 3], table_rows)
    for s in range(2):
        for f in range(6):
            d = f % 3
            if f < 3:
                own = modes[s, f]
                value = rhs[s, f]
                if d == 2 and s == 0:
                    other = tilde_low[1, 2]
                else:
                    base = 24 * s if d < 2 else 0
                    other = to_upper_order(plus[d][base + 16 : base + 22, :], up_perm[s, d])
            else:
                own = tilde_low[s, d]
                if d == 2 and s == 1:
                    other = modes[0, 2]
                    value = rhs[0, 2]
                else:
                    base = 24 * s if d < 2 else 0
                    other = minus[d][base + 16 : base + 22, :]
                    inside = lax.axis_index(AXES[d]) > 0
                    value = minus[d][base : base + 16, :] * inside.astype(f32)
            start[s, f] = value
            work[...] = jnp.zeros(work.shape, f32)
            work[own_slot(s) * SLOT : own_slot(s) * SLOT + 8, :] = jnp.concatenate([own, zero2], 0)
            n = nbr_slot(s, f)
            work[n * SLOT : n * SLOT + 8, :] = jnp.concatenate([other, zero2], 0)
            both = split2(work[...])
            lift[s * 6 + f] = both
            partial[s] += mm(split3(value), both, NT)

    rows[...] = jnp.zeros(rows.shape, f32)
    pieces = [(2, minus[0], 48, 16), (4, plus[0], 48, 16), (6, minus[1], 48, 16), (8, plus[1], 48, 16)]
    pieces += [(10, minus[2], 24 + 8, 8), (11, plus[2], 24, 8)]
    for k in range(slabs):
        width = min(256, coarse.shape[1] - 256 * k)
        slab = coarse[:, 256 * k : 256 * k + width]
        if width < 256:
            slab = jnp.concatenate([slab, jnp.zeros((12, 256 - width), f32)], 1)
        slab = jnp.concatenate([slab[:6], zero2, slab[6:], zero2], 0)
        rows[0:16, 256 * k : 256 * k + 256] = slab
        for slot, source, base, count in pieces:
            rows[slot * SLOT : slot * SLOT + count, 256 * k : 256 * k + 256] = source[
                base + 16 * k : base + 16 * k + count, :
            ]
    both = split2(rows[...])
    index_row = lax.broadcasted_iota(jnp.int32, (256 * slabs, LANES), 0)
    line = lax.broadcasted_iota(jnp.int32, (LANES, LANES), 0)
    column = lax.broadcasted_iota(jnp.int32, (LANES, LANES), 1)
    passing = ((line == column) & (line >= RHO) & (line <= FD)).astype(f32)
    total = [fold3(part) for part in partial]
    total = [part[:, :LANES] + part[:, LANES:] for part in total]
    lane = lax.broadcasted_iota(jnp.int32, total[0].shape, 1)
    total = jnp.where(lane < SLOT, total[0], jnp.where(lane < 2 * SLOT, total[1], 0.0))

    def build(q2, carry):
        halves = []
        for q in range(2):
            choose = (index_row == table[2 * q2 + q]).astype(bf16)
            got = mm(both, choose, NN)
            halves.append(jnp.concatenate([got[:LANES] + passing, got[LANES:]], 0))
        solve[q2] = jnp.concatenate(halves, 1).astype(bf16)
        return carry

    lax.fori_loop(0, devices // 2, build, 0)
    spread_out(total, solve, send)


def spread_out(part, solve, send):
    left = split3(part)
    left = jnp.concatenate([left, left], 1)
    pairs = solve.shape[0]

    def one(q2):
        got = fold3(mm(left, solve[q2], NN))
        send[2 * q2] = got[:, :LANES]
        send[2 * q2 + 1] = got[:, LANES:]

    if pairs <= 16:
        for q2 in range(pairs):
            one(q2)
    else:

        def step(q2, carry):
            one(q2)
            return carry

        lax.fori_loop(0, pairs, step, 0)


def gather_sum(recv):
    devices = recv.shape[0]
    if devices <= 32:
        parts = [recv[q] for q in range(devices)]
        while len(parts) > 1:
            parts = [parts[i] + parts[i + 1] for i in range(0, len(parts), 2)]
        return parts[0]
    return lax.fori_loop(0, devices, lambda q, acc: acc + recv[q], jnp.zeros(recv.shape[1:], f32))


def lift_left(total):
    left = split3(total)
    return jnp.concatenate([left, left], 1)


def apply_factors(residual, pattern, factors, perm, lift, masks, parity, previous, forward, image, solve, sends):
    xa, xb, ya, yb, za, zb, send = sends
    partial = jnp.zeros((48, 256), f32)
    own_sum = jnp.zeros((16, 256), f32)
    square = jnp.zeros((16, 256), f32)
    cross = jnp.zeros((16, 256), f32)
    faces = {}
    for s in range(2):
        sides = []
        for j in range(6):
            value = residual[s][j]
            if j < 3:
                own_sum += value * value
                sides.append(split2(value))
            else:
                sides.append((-mm(split2(value), perm[s * 3 + j - 3], NN)).astype(bf16))
        present = [[pattern[s, i, j].astype(f32).astype(bf16) for j in range(6)] for i in range(6)]
        halves = []
        for i in range(6):
            acc = jnp.zeros((32, 256), f32)
            for j in range(6):
                acc += mm(sides[j] * present[i][j], factors[s, i, j], NT)
            got = fold2(acc)
            forward[s, i] = got
            square += got * got
            if previous is not None:
                cross += got * previous[s][i]
            halves.append(split2(got))
        for j in range(6):
            acc = jnp.zeros((32, 256), f32)
            for i in range(6):
                acc += mm(halves[i] * present[i][j], factors[s, i, j], NN)
            got = fold2(acc)
            if j >= 3:
                got = -fold3(mm(split3(got), perm[s * 3 + j - 3], NT))
            got = masked(got, masks[s][j])
            image[s, j] = got
            faces[s, j] = got
            partial += mm(split3(got), lift[s * 6 + j], NT)
    for s in range(2):
        xa[s] = pick(parity[0], faces[s, 3], faces[s, 0])
        xb[s] = pick(parity[0], faces[s, 0], faces[s, 3])
        ya[s] = pick(parity[1], faces[s, 4], faces[s, 1])
        yb[s] = pick(parity[1], faces[s, 1], faces[s, 4])
    za[...] = pick(parity[2], faces[0, 5], faces[1, 2])
    zb[...] = pick(parity[2], faces[1, 2], faces[0, 5])
    total = fold3(partial)
    total = total[:, :LANES] + total[:, LANES:]
    lane = lax.broadcasted_iota(jnp.int32, total.shape, 1)
    for where, values in ((RHO, own_sum), (FF, square), (FD, cross)):
        total = jnp.where(lane == where, jnp.sum(values, axis=1, keepdims=True), total)
    spread_out(total, solve, send)


def first_kernel(sizes, pattern, recv, start, factors, perm, lift, solve, residual, forward, image, *sends):
    parity, masks = position(sizes)
    left = lift_left(gather_sum(recv))
    now = [[None] * 6 for _ in range(2)]
    for s in range(2):
        for f in range(6):
            value = start[s, f] - masked(fold3(mm(left, lift[s * 6 + f], NN)), masks[s][f])
            residual[s, f] = value
            now[s][f] = value
    apply_factors(now, pattern, factors, perm, lift, masks, parity, None, forward, image, solve, sends)


def update(sizes, first, recvs, state, count):
    parity, masks = position(sizes)
    xa, xb, ya, yb, za, zb, recv = recvs
    residual, forward, image, lift, old = state
    total = gather_sum(recv)
    left = lift_left(total)
    sums = jnp.sum(total, axis=0, keepdims=True)
    lane = lax.broadcasted_iota(jnp.int32, sums.shape, 1)

    def scalar(at):
        return jnp.sum(jnp.where(lane == at, sums, 0.0), axis=1, keepdims=True)

    rho, curvature = scalar(RHO), scalar(FF)
    if first:
        beta = None
    else:
        direction, moved, along, multipliers, scalars = old
        beta = rho / scalars[0:1, 0:1]
        curvature = curvature + 2.0 * beta * scalar(FD) + beta * beta * scalars[1:2, 0:1]
    step = rho / curvature
    out = {}
    for s in range(2):
        for f in range(count):
            d = f % 3
            if d == 2 and (s == 0) == (f == 2):
                other = image[1 - s, 5 if f == 2 else 2]
            else:
                a, b = ((xa, xb), (ya, yb), (za, zb))[d]
                va = a[s] if d < 2 else a[...]
                vb = b[s] if d < 2 else b[...]
                other = pick(parity[d], vb, va) if f < 3 else pick(parity[d], va, vb)
            change = image[s, f] + other - fold3(mm(left, lift[s * 6 + f], NN))
            change = masked(change, masks[s][f])
            value = residual[s, f]
            towards = value
            if not first:
                towards = value + beta * direction[s, f]
                change = change + beta * moved[s, f]
            out[s, f] = (value - step * change, towards, change)
            if f < 3:
                gain = step * towards
                out[s, f] += (gain if first else multipliers[s, f] + gain,)
    return parity, masks, beta, rho, curvature, out


def middle_kernel(sizes, first, *refs):
    pattern, factors, perm, lift, solve = refs[:5]
    recvs = refs[5:12]
    residual, forward, image = refs[12:15]
    rest = refs[15:]
    if first:
        old = None
    else:
        old, rest = rest[:5], rest[5:]
    new_residual, new_forward, new_image, new_direction, new_moved, new_along, new_multipliers, new_scalars = rest[:8]
    sends = rest[8:]
    parity, masks, beta, rho, curvature, out = update(
        sizes, first, recvs, (residual, forward, image, lift, old), 6
    )
    row = lax.broadcasted_iota(jnp.int32, (8, LANES), 0)
    new_scalars[...] = jnp.where(row == 0, rho, curvature)
    now = [[None] * 6 for _ in range(2)]
    along = [[None] * 6 for _ in range(2)]
    for s in range(2):
        for f in range(6):
            values = out[s, f]
            now[s][f] = values[0]
            new_residual[s, f] = values[0]
            new_direction[s, f] = values[1]
            new_moved[s, f] = values[2]
            if f < 3:
                new_multipliers[s, f] = values[3]
            line = forward[s, f] if first else forward[s, f] + beta * old[2][s, f]
            along[s][f] = line
            new_along[s, f] = line
    apply_factors(now, pattern, factors, perm, lift, masks, parity, along, new_forward, new_image, solve, sends)


def last_kernel(sizes, lift, *refs):
    recvs = refs[:7]
    residual, forward, image = refs[7:10]
    old = refs[10:15]
    multipliers, final = refs[15:]
    out = update(sizes, False, recvs, (residual, forward, image, lift, old), 3)[5]
    for s in range(2):
        for f in range(3):
            final[s, f] = out[s, f][0]
            multipliers[s, f] = out[s, f][3]


def exchange(values, axis):
    size = lax.axis_size(axis)
    first = lax.ppermute(values[0], axis, [(i, i ^ 1) for i in range(size)])
    if size == 2:
        return first, first
    second = lax.ppermute(
        values[1], axis, [(i, (i + 1) % size if i % 2 else (i - 1) % size) for i in range(size)]
    )
    return first, second


def communicate(sends):
    xa, xb, ya, yb, za, zb, send = sends
    recv = lax.all_to_all(send, AXES, 0, 0, tiled=True)
    za, zb = exchange((za, zb), "gz")
    xa, xb = exchange((xa, xb), "gx")
    ya, yb = exchange((ya, yb), "gy")
    return xa, xb, ya, yb, za, zb, recv


def per_device(dual_rhs, factors, block_pattern, face_map, rigid_modes, coarse_solve):
    sizes = tuple(lax.axis_size(a) for a in AXES)
    devices = sizes[0] * sizes[1] * sizes[2]
    cases, dofs = dual_rhs.shape[4:]
    nc = coarse_solve.shape[1]
    slabs = -(-nc // 256)
    rhs = dual_rhs.reshape(dual_rhs.shape[2:])
    factors = factors.reshape(factors.shape[2:])
    pattern = block_pattern.reshape(block_pattern.shape[2:])
    fmap = face_map.reshape(face_map.shape[2:])
    modes = rigid_modes.reshape(rigid_modes.shape[2:])
    vmem = pl.BlockSpec(memory_space=pltpu.VMEM)
    smem = pl.BlockSpec(memory_space=pltpu.SMEM)
    params = pltpu.CompilerParams(vmem_limit_bytes=24 << 20)

    def shape(*dims, dtype=f32):
        return jax.ShapeDtypeStruct(dims, dtype)

    def call(kernel, outs, ins, first_smem=False, scratch=()):
        specs = [smem if i == 0 and first_smem else vmem for i in range(len(ins))]
        return pl.pallas_call(
            kernel,
            out_shape=outs,
            in_specs=specs,
            out_specs=[vmem] * len(outs),
            scratch_shapes=list(scratch),
            compiler_params=params,
        )(*ins)

    packs = [shape(48 + 16 * slabs, dofs)] * 4 + [shape(24 + 16 * slabs, dofs)] * 2
    xa, xb, ya, yb, za, zb = call(pack_kernel, packs, [rhs, modes, fmap, coarse_solve])
    za, zb = exchange((za, zb), "gz")
    xa, xb = exchange((xa, xb), "gx")
    ya, yb = exchange((ya, yb), "gy")

    table = jnp.asarray(slot_table(*sizes, nc)).reshape(devices, 1, LANES)
    faces = shape(2, 6, cases, dofs)
    sent = shape(devices, cases, LANES)
    perm, lift, start, solve, send = call(
        setup_kernel,
        [
            shape(6, dofs, dofs, dtype=bf16),
            shape(12, 2 * LANES, dofs, dtype=bf16),
            faces,
            shape(devices // 2, 2 * LANES, 2 * LANES, dtype=bf16),
            sent,
        ],
        [rhs, modes, fmap, coarse_solve, table, xa, xb, ya, yb, za, zb],
        scratch=(pltpu.VMEM((LANES, dofs), f32), pltpu.VMEM((LANES, 256 * slabs), f32)),
    )
    recv = lax.all_to_all(send, AXES, 0, 0, tiled=True)

    sends = [shape(2, cases, dofs)] * 4 + [shape(cases, dofs)] * 2 + [sent]
    residual, forward, image, *out = call(
        functools.partial(first_kernel, sizes),
        [faces, faces, faces] + sends,
        [pattern, recv, start, factors, perm, lift, solve],
        first_smem=True,
    )
    old = []
    for iteration in range(ITERS - 1):
        got = communicate(out)
        residual, forward, image, *out = call(
            functools.partial(middle_kernel, sizes, iteration == 0),
            [faces] * 6 + [shape(2, 3, cases, dofs), shape(8, LANES)] + sends,
            [pattern, factors, perm, lift, solve, *got, residual, forward, image, *old],
            first_smem=True,
        )
        old, out = out[:5], out[5:]
    got = communicate(out)
    multipliers, final = call(
        functools.partial(last_kernel, sizes),
        [shape(2, 3, cases, dofs)] * 2,
        [lift, *got, residual, forward, image, *old],
    )
    return multipliers.reshape(dual_rhs.shape), final.reshape(dual_rhs.shape)


def solution(mesh):
    return jax.shard_map(
        per_device,
        mesh=mesh,
        in_specs=(
            P("gx", "gy", "gz", None, None, None),
            P("gx", "gy", "gz", None, None, None, None),
            P("gx", "gy", "gz", None, None),
            P("gx", "gy", "gz", None, None),
            P("gx", "gy", "gz", None, None, None),
            P(("gx", "gy", "gz"), None),
        ),
        out_specs=(P("gx", "gy", "gz", None, None, None), P("gx", "gy", "gz", None, None, None)),
        check_vma=False,
    )
```

```python
import functools

import jax
import jax.numpy as jnp
from jax import lax
from jax.experimental import pallas as pl
from jax.experimental.pallas import tpu as pltpu
from jax.sharding import PartitionSpec as P

ITERS = 4
AXES = ("gx", "gy", "gz")
LANES = 128
SLOT = 8
SLOTS = 12
SCALARS = 3
NT = (((1,), (1,)), ((), ()))
NN = (((1,), (0,)), ((), ()))
f32 = jnp.float32
bf16 = jnp.bfloat16


def own_slot(s):
    return s


COLUMN_OF_FACE = {0: 2, 3: 1, 1: 4, 4: 3}


def whole_lanes(nc):
    return -(-(nc + SCALARS) // 256) * 256


def column_lanes(levels):
    return -(-(30 * levels + SCALARS) // LANES) * LANES


def nbr_slot(s, f):
    if f == 0:
        return 4 + s
    if f == 3:
        return 2 + s
    if f == 1:
        return 8 + s
    if f == 4:
        return 6 + s
    if f == 2:
        return 1 if s == 0 else 11
    return 10 if s == 0 else 0


def split2(x):
    high = x.astype(bf16)
    low = (x - high.astype(f32)).astype(bf16)
    return jnp.concatenate([high, low], 0)


def split3(x):
    high = x.astype(bf16)
    rest = x - high.astype(f32)
    mid = rest.astype(bf16)
    low = (rest - mid.astype(f32)).astype(bf16)
    return jnp.concatenate([high, mid, low], 0)


def fold2(x):
    n = x.shape[0] // 2
    return x[:n] + x[n:]


def fold3(x):
    n = x.shape[0] // 3
    return x[:n] + (x[n : 2 * n] + x[2 * n :])


def mm(a, b, dims):
    return lax.dot_general(a, b, dims, preferred_element_type=f32)


def position(sizes):
    index = [lax.axis_index(a) for a in AXES]
    parity = [lax.rem(i, 2) == 1 for i in index]
    masks = []
    for s in range(2):
        row = []
        for f in range(6):
            d = f % 3
            if d == 2 and (s == 0) == (f == 2):
                row.append(None)
            else:
                inside = (index[d] < sizes[d] - 1) if f < 3 else (index[d] > 0)
                row.append(inside.astype(f32))
        masks.append(row)
    return parity, masks


def masked(value, mask):
    return value if mask is None else value * mask


def pick(cond, a, b):
    return jnp.where(cond, a, b)


def pack_kernel(rhs, modes, fmap, coarse, xa, xb, ya, yb, za, zb):
    parity, _ = position((1, 1, 1))
    slabs = -(-coarse.shape[1] // 256)
    for d, outs in ((0, (xa, xb)), (1, (ya, yb))):
        for s in range(2):
            up, down = modes[s, d], modes[s, d + 3]
            first = pick(parity[d], down, up)
            second = pick(parity[d], up, down)
            for out, piece in zip(outs, (first, second)):
                out[24 * s : 24 * s + 16, :] = rhs[s, d]
                out[24 * s + 16 : 24 * s + 24, :] = jnp.concatenate(
                    [piece, fmap[s, d : d + 1, :].astype(f32), jnp.zeros((1, 256), f32)], 0
                )
    up, down = modes[1, 2], modes[0, 5]
    for out, piece in zip((za, zb), (pick(parity[2], down, up), pick(parity[2], up, down))):
        out[0:16, :] = rhs[1, 2]
        out[16:24, :] = jnp.concatenate([piece, fmap[1, 2:3, :].astype(f32), jnp.zeros((1, 256), f32)], 0)
    for k in range(slabs):
        width = min(256, coarse.shape[1] - 256 * k)
        slab = coarse[:, 256 * k : 256 * k + width]
        if width < 256:
            slab = jnp.concatenate([slab, jnp.zeros((12, 256 - width), f32)], 1)
        gap = jnp.zeros((2, 256), f32)
        slab = jnp.concatenate([slab[:6], gap, slab[6:], gap], 0)
        for out, base in ((xa, 48), (xb, 48), (ya, 48), (yb, 48), (za, 24), (zb, 24)):
            out[base + 16 * k : base + 16 * k + 16, :] = slab


def setup_kernel(sizes, rhs, modes, fmap, coarse, xa, xb, ya, yb, za, zb, perm, lift, sums, start, solve, place, part, work, rows):
    parity, _ = position((1, 1, 1))
    nc = coarse.shape[1]
    slabs = -(-nc // 256)
    levels = 2 * sizes[2]
    lanes = column_lanes(levels)
    gx, gy, gz = (lax.axis_index(a) for a in AXES)
    lane_row = lax.broadcasted_iota(jnp.int32, (256, 256), 0)

    plus, minus = [], []
    for d, (a, b) in enumerate(((xa, xb), (ya, yb), (za, zb))):
        va, vb = a[...], b[...]
        plus.append(pick(parity[d], vb, va))
        minus.append(pick(parity[d], va, vb))

    def onehot(row):
        return (lane_row == row.astype(jnp.int32)).astype(bf16)

    def to_upper_order(values, table_rows):
        return -fold3(mm(split3(values), table_rows, NT))

    zero2 = jnp.zeros((2, 256), f32)
    partial = jnp.zeros((48, lanes), f32)
    lane_column = lax.broadcasted_iota(jnp.int32, (lanes, 16), 0)
    source_row = lax.broadcasted_iota(jnp.int32, (lanes, 16), 1)
    up_perm = {}
    for s in range(2):
        for d in range(3):
            up_perm[s, d] = onehot(fmap[s, d : d + 1, :])
    tilde_low = {}
    for s in range(2):
        for d in range(3):
            if d == 2 and s == 1:
                table_rows = up_perm[0, 2]
            else:
                base = 24 * s if d < 2 else 0
                table_rows = onehot(minus[d][base + 22 : base + 23, :])
            perm[s * 3 + d] = table_rows
            tilde_low[s, d] = to_upper_order(modes[s, d + 3], table_rows)
    for s in range(2):
        for f in range(6):
            d = f % 3
            if f < 3:
                own = modes[s, f]
                value = rhs[s, f]
                if d == 2 and s == 0:
                    other = tilde_low[1, 2]
                else:
                    base = 24 * s if d < 2 else 0
                    other = to_upper_order(plus[d][base + 16 : base + 22, :], up_perm[s, d])
            else:
                own = tilde_low[s, d]
                if d == 2 and s == 1:
                    other = modes[0, 2]
                    value = rhs[0, 2]
                else:
                    base = 24 * s if d < 2 else 0
                    other = minus[d][base + 16 : base + 22, :]
                    inside = lax.axis_index(AXES[d]) > 0
                    value = minus[d][base : base + 16, :] * inside.astype(f32)
            start[s, f] = value
            work[...] = jnp.zeros(work.shape, f32)
            work[own_slot(s) * SLOT : own_slot(s) * SLOT + 8, :] = jnp.concatenate([own, zero2], 0)
            n = nbr_slot(s, f)
            work[n * SLOT : n * SLOT + 8, :] = jnp.concatenate([other, zero2], 0)
            lift[s * 6 + f] = split2(work[...])
            pair = split2(jnp.concatenate([own, zero2, other, zero2], 0))
            level = 2 * gz + s
            if d == 2:
                target = (level + (1 if f == 2 else -1)) * 6
            else:
                target = COLUMN_OF_FACE[f] * 6 * levels + level * 6
            mode = jnp.bitwise_and(source_row, 7)
            aim = jnp.where(source_row < 8, level * 6, target) + mode
            choose = (lane_column == aim) & (mode < 6)
            both = choose.astype(bf16)
            alone = (choose & (source_row < 8)).astype(bf16)
            left = split3(value)
            for h in range(2):
                half = pair[16 * h : 16 * h + 16]
                sums[s * 6 + f, h * lanes : h * lanes + lanes, :] = mm(both, half, NN).astype(bf16)
                partial += mm(left, mm(alone, half, NN).astype(bf16), NT)

    rows[...] = jnp.zeros(rows.shape, f32)
    pieces = [(2, minus[0], 48, 16), (4, plus[0], 48, 16), (6, minus[1], 48, 16), (8, plus[1], 48, 16)]
    pieces += [(10, minus[2], 24 + 8, 8), (11, plus[2], 24, 8)]
    for k in range(slabs):
        width = min(256, coarse.shape[1] - 256 * k)
        slab = coarse[:, 256 * k : 256 * k + width]
        if width < 256:
            slab = jnp.concatenate([slab, jnp.zeros((12, 256 - width), f32)], 1)
        slab = jnp.concatenate([slab[:6], zero2, slab[6:], zero2], 0)
        rows[0:16, 256 * k : 256 * k + 256] = slab
        for slot, source, base, count in pieces:
            rows[slot * SLOT : slot * SLOT + count, 256 * k : 256 * k + 256] = source[
                base + 16 * k : base + 16 * k + count, :
            ]
    solve[...] = split2(rows[...])
    line = lax.broadcasted_iota(jnp.int32, (lanes, 1), 0)
    whole = lax.broadcasted_iota(jnp.int32, (lanes, place.shape[1]), 1)
    for k in range(sizes[1]):
        y = jnp.bitwise_xor(gy, k)
        aim = jnp.where(line >= 30 * levels, nc + line - 30 * levels, -1)
        for t, (dx, dy) in enumerate(((0, 0), (-1, 0), (1, 0), (0, -1), (0, 1))):
            inside = (gx + dx >= 0) & (gx + dx < sizes[0]) & (y + dy >= 0) & (y + dy < sizes[1])
            first = jnp.where(inside, ((gx + dx) * sizes[1] + y + dy - t) * 6 * levels, -6 * nc)
            aim = jnp.where((line >= t * 6 * levels) & (line < (t + 1) * 6 * levels), line + first, aim)
        place[k * lanes : k * lanes + lanes, :] = (whole == aim).astype(bf16)
    part[...] = fold3(partial)


def tail(ref, lanes):
    return ref[:, ref.shape[1] - lanes :]


def beside(outs, faces, values):
    if faces:
        for out, face in zip(outs, faces):
            width = face.shape[1]
            out[:, :width] = face[...]
            out[:, width:] = values
    outs[-1][...] = values


def column_kernel(count, *refs):
    lanes = refs[0].shape[1]
    total = refs[0][...]
    for part in refs[1:count]:
        total += tail(part, lanes)
    split = count + (len(refs) - count) // 2
    beside(refs[split:], refs[count:split], total)


def place_kernel(count, place, *refs):
    lanes = refs[0].shape[1]
    left = jnp.concatenate([split3(tail(part, lanes)) for part in refs[:count]], 1)
    split = count + (len(refs) - count) // 2
    beside(refs[split:], refs[count:split], fold3(mm(left, place[...], NN)))


def coarse(whole, parts, solve):
    total = whole[...]
    for part in parts:
        total += tail(part, whole.shape[1])
    got = fold3(mm(split3(total[:, : solve.shape[1]]), solve[...], NT))
    return total, got[:, :LANES] + got[:, LANES:]


def lift_left(total):
    left = split3(total)
    return jnp.concatenate([left, left], 1)


def apply_factors(residual, pattern, factors, perm, sums, masks, parity, previous, forward, image, sends):
    xa, xb, ya, yb, za, zb, part = sends
    lanes = part.shape[1]
    partial = jnp.zeros((48, 2 * lanes), f32)
    own_sum = jnp.zeros((16, 256), f32)
    square = jnp.zeros((16, 256), f32)
    cross = jnp.zeros((16, 256), f32)
    faces = {}
    for s in range(2):
        sides = []
        for j in range(6):
            value = residual[s][j]
            if j < 3:
                own_sum += value * value
                sides.append(split2(value))
            else:
                sides.append((-mm(split2(value), perm[s * 3 + j - 3], NN)).astype(bf16))
        present = [[pattern[s, i, j].astype(f32).astype(bf16) for j in range(6)] for i in range(6)]
        halves = []
        for i in range(6):
            acc = jnp.zeros((32, 256), f32)
            for j in range(6):
                acc += mm(sides[j] * present[i][j], factors[s, i, j], NT)
            got = fold2(acc)
            forward[s, i] = got
            square += got * got
            if previous is not None:
                cross += got * previous[s][i]
            halves.append(split2(got))
        for j in range(6):
            acc = jnp.zeros((32, 256), f32)
            for i in range(6):
                acc += mm(halves[i] * present[i][j], factors[s, i, j], NN)
            got = fold2(acc)
            if j >= 3:
                got = -fold3(mm(split3(got), perm[s * 3 + j - 3], NT))
            got = masked(got, masks[s][j])
            image[s, j] = got
            faces[s, j] = got
            partial += mm(split3(got), sums[s * 6 + j], NT)
    for s in range(2):
        at = slice(256 * s, 256 * s + 256)
        xa[:, at] = pick(parity[0], faces[s, 3], faces[s, 0])
        xb[:, at] = pick(parity[0], faces[s, 0], faces[s, 3])
        ya[:, at] = pick(parity[1], faces[s, 4], faces[s, 1])
        yb[:, at] = pick(parity[1], faces[s, 1], faces[s, 4])
    total = fold3(partial)
    total = total[:, :lanes] + total[:, lanes:]
    lane = lax.broadcasted_iota(jnp.int32, total.shape, 1)
    scalars = 30 * 2 * lax.axis_size("gz")
    for k, values in enumerate((own_sum, square, cross)):
        total = jnp.where(lane == scalars + k, jnp.sum(values, axis=1, keepdims=True), total)
    part[...] = total
    for out, face in ((za, pick(parity[2], faces[0, 5], faces[1, 2])), (zb, pick(parity[2], faces[1, 2], faces[0, 5]))):
        out[:, :256] = face
        out[:, 256:] = total


def first_kernel(sizes, count, pattern, factors, perm, lift, sums, solve, start, *refs):
    parity, masks = position(sizes)
    residual, forward, image = refs[count : count + 3]
    left = lift_left(coarse(refs[0], refs[1:count], solve)[1])
    now = [[None] * 6 for _ in range(2)]
    for s in range(2):
        for f in range(6):
            value = start[s, f] - masked(fold3(mm(left, lift[s * 6 + f], NN)), masks[s][f])
            residual[s, f] = value
            now[s][f] = value
    apply_factors(now, pattern, factors, perm, sums, masks, parity, None, forward, image, refs[count + 3 :])


def update(sizes, nc, first, faces, parts, state, count):
    parity, masks = position(sizes)
    residual, forward, image, lift, solve, old = state
    total, solution_part = coarse(parts[0], parts[1:], solve)
    left = lift_left(solution_part)
    sums = jnp.sum(total, axis=0, keepdims=True)
    lane = lax.broadcasted_iota(jnp.int32, sums.shape, 1)

    def scalar(k):
        return jnp.sum(jnp.where(lane == nc + k, sums, 0.0), axis=1, keepdims=True)

    rho, curvature = scalar(0), scalar(1)
    if first:
        beta = None
    else:
        direction, moved, along, multipliers, scalars = old
        beta = rho / scalars[0:1, 0:1]
        curvature = curvature + 2.0 * beta * scalar(2) + beta * beta * scalars[1:2, 0:1]
    step = rho / curvature
    out = {}
    for s in range(2):
        for f in range(count):
            d = f % 3
            if d == 2 and (s == 0) == (f == 2):
                other = image[1 - s, 5 if f == 2 else 2]
            else:
                at = 256 * s if d < 2 else 0
                va, vb = (face[:, at : at + 256] for face in faces[2 * d : 2 * d + 2])
                other = pick(parity[d], vb, va) if f < 3 else pick(parity[d], va, vb)
            change = image[s, f] + other - fold3(mm(left, lift[s * 6 + f], NN))
            change = masked(change, masks[s][f])
            value = residual[s, f]
            towards = value
            if not first:
                towards = value + beta * direction[s, f]
                change = change + beta * moved[s, f]
            out[s, f] = (value - step * change, towards, change)
            if f < 3:
                gain = step * towards
                out[s, f] += (gain if first else multipliers[s, f] + gain,)
    return parity, masks, beta, rho, curvature, out


def middle_kernel(sizes, nc, first, count, *refs):
    pattern, factors, perm, lift, sums, solve = refs[:6]
    faces, parts = refs[6:12], refs[12 : 12 + count]
    residual, forward, image = refs[12 + count : 15 + count]
    rest = refs[15 + count :]
    if first:
        old = None
    else:
        old, rest = rest[:5], rest[5:]
    new_residual, new_forward, new_image, new_direction, new_moved, new_along, new_multipliers, new_scalars = rest[:8]
    parity, masks, beta, rho, curvature, out = update(
        sizes, nc, first, faces, parts, (residual, forward, image, lift, solve, old), 6
    )
    row = lax.broadcasted_iota(jnp.int32, (8, LANES), 0)
    new_scalars[...] = jnp.where(row == 0, rho, curvature)
    now = [[None] * 6 for _ in range(2)]
    along = [[None] * 6 for _ in range(2)]
    for s in range(2):
        for f in range(6):
            values = out[s, f]
            now[s][f] = values[0]
            new_residual[s, f] = values[0]
            new_direction[s, f] = values[1]
            new_moved[s, f] = values[2]
            if f < 3:
                new_multipliers[s, f] = values[3]
            line = forward[s, f] if first else forward[s, f] + beta * old[2][s, f]
            along[s][f] = line
            new_along[s, f] = line
    apply_factors(now, pattern, factors, perm, sums, masks, parity, along, new_forward, new_image, rest[8:])


def last_kernel(sizes, nc, count, lift, solve, *refs):
    faces, parts = refs[:6], refs[6 : 6 + count]
    residual, forward, image = refs[6 + count : 9 + count]
    old = refs[9 + count : 14 + count]
    multipliers, final = refs[14 + count :]
    out = update(sizes, nc, False, faces, parts, (residual, forward, image, lift, solve, old), 3)[5]
    for s in range(2):
        for f in range(3):
            final[s, f] = out[s, f][0]
            multipliers[s, f] = out[s, f][3]


def swap(values, axis, distance):
    return lax.ppermute(values, axis, [(i, i ^ distance) for i in range(lax.axis_size(axis))])


def exchange(first, second, axis, alone=None):
    size = lax.axis_size(axis)
    below = swap(first, axis, 1)
    if size == 2:
        return below, below, [below]
    above = lax.ppermute(second, axis, [(i, (i + 1) % size if i % 2 else (i - 1) % size) for i in range(size)])
    others = [below]
    if alone is not None:
        for distance in range(2, size):
            others.append(above if size == 4 and distance == 3 else swap(alone, axis, distance))
    return below, above, others


def per_device(dual_rhs, factors, block_pattern, face_map, rigid_modes, coarse_solve):
    sizes = tuple(lax.axis_size(a) for a in AXES)
    cases, dofs = dual_rhs.shape[4:]
    nc = coarse_solve.shape[1]
    slabs = -(-nc // 256)
    rhs = dual_rhs.reshape(dual_rhs.shape[2:])
    factors = factors.reshape(factors.shape[2:])
    pattern = block_pattern.reshape(block_pattern.shape[2:])
    fmap = face_map.reshape(face_map.shape[2:])
    modes = rigid_modes.reshape(rigid_modes.shape[2:])
    vmem = pl.BlockSpec(memory_space=pltpu.VMEM)
    smem = pl.BlockSpec(memory_space=pltpu.SMEM)
    table_bytes = 2 * sizes[1] * column_lanes(2 * sizes[2]) * whole_lanes(nc)
    params = pltpu.CompilerParams(vmem_limit_bytes=(16 << 20) + table_bytes)

    def shape(*dims, dtype=f32):
        return jax.ShapeDtypeStruct(dims, dtype)

    def call(kernel, outs, ins, first_smem=False, scratch=()):
        specs = [smem if i == 0 and first_smem else vmem for i in range(len(ins))]
        return pl.pallas_call(
            kernel,
            out_shape=outs,
            in_specs=specs,
            out_specs=[vmem] * len(outs),
            scratch_shapes=list(scratch),
            compiler_params=params,
        )(*ins)

    levels = 2 * sizes[2]
    lanes, whole = column_lanes(levels), whole_lanes(nc)
    packs = [shape(48 + 16 * slabs, dofs)] * 4 + [shape(24 + 16 * slabs, dofs)] * 2
    xa, xb, ya, yb, za, zb = call(pack_kernel, packs, [rhs, modes, fmap, coarse_solve])
    za, zb, _ = exchange(za, zb, "gz")
    xa, xb, _ = exchange(xa, xb, "gx")
    ya, yb, _ = exchange(ya, yb, "gy")
    faces = shape(2, 6, cases, dofs)
    perm, lift, sums, start, solve, place, part = call(
        functools.partial(setup_kernel, sizes),
        [
            shape(6, dofs, dofs, dtype=bf16),
            shape(12, 2 * LANES, dofs, dtype=bf16),
            shape(12, 2 * lanes, dofs, dtype=bf16),
            faces,
            shape(2 * LANES, 256 * slabs, dtype=bf16),
            shape(sizes[1] * lanes, whole, dtype=bf16),
            shape(cases, lanes),
        ],
        [rhs, modes, fmap, coarse_solve, xa, xb, ya, yb, za, zb],
        scratch=(pltpu.VMEM((LANES, dofs), f32), pltpu.VMEM((LANES, 256 * slabs), f32)),
    )

    def reduce(part, za, zb, along_y, along_x):
        za, zb, others = exchange(za, zb, "gz", part)
        outs = [shape(cases, face.shape[1] + lanes) for face in along_y] + [shape(cases, lanes)]
        ins = [part, *others, *along_y]
        *along_y, part = call(functools.partial(column_kernel, 1 + len(others)), outs, ins)
        ya, yb, others = exchange(*(along_y or (part, part)), "gy", part)
        outs = [shape(cases, face.shape[1] + whole) for face in along_x] + [shape(cases, whole)]
        ins = [place, part, *others, *along_x]
        *along_x, part = call(functools.partial(place_kernel, 1 + len(others)), outs, ins)
        xa, xb, others = exchange(*(along_x or (part, part)), "gx", part)
        return [xa, xb, ya, yb, za, zb], [part, *others]

    parts = reduce(part, part, part, (), ())[1]
    wide = shape(cases, 2 * dofs)
    sends = [wide] * 4 + [shape(cases, dofs + lanes)] * 2 + [shape(cases, lanes)]
    residual, forward, image, *out = call(
        functools.partial(first_kernel, sizes, len(parts)),
        [faces, faces, faces] + sends,
        [pattern, factors, perm, lift, sums, solve, start, *parts],
        first_smem=True,
    )
    old = []
    for iteration in range(ITERS - 1):
        xa, xb, ya, yb, za, zb, part = out
        got, parts = reduce(part, za, zb, (ya, yb), (xa, xb))
        residual, forward, image, *out = call(
            functools.partial(middle_kernel, sizes, nc, iteration == 0, len(parts)),
            [faces] * 6 + [shape(2, 3, cases, dofs), shape(8, LANES)] + sends,
            [pattern, factors, perm, lift, sums, solve, *got, *parts, residual, forward, image, *old],
            first_smem=True,
        )
        old, out = out[:5], out[5:]
    xa, xb, ya, yb, za, zb, part = out
    got, parts = reduce(part, za, zb, (ya, yb), (xa, xb))
    multipliers, final = call(
        functools.partial(last_kernel, sizes, nc, len(parts)),
        [shape(2, 3, cases, dofs)] * 2,
        [lift, solve, *got, *parts, residual, forward, image, *old],
    )
    return multipliers.reshape(dual_rhs.shape), final.reshape(dual_rhs.shape)


def solution(mesh):
    return jax.shard_map(
        per_device,
        mesh=mesh,
        in_specs=(
            P("gx", "gy", "gz", None, None, None),
            P("gx", "gy", "gz", None, None, None, None),
            P("gx", "gy", "gz", None, None),
            P("gx", "gy", "gz", None, None),
            P("gx", "gy", "gz", None, None, None),
            P(("gx", "gy", "gz"), None),
        ),
        out_specs=(P("gx", "gy", "gz", None, None, None), P("gx", "gy", "gz", None, None, None)),
        check_vma=False,
    )
```

```python
import functools

import jax
import jax.numpy as jnp
from jax import lax
from jax.experimental import pallas as pl
from jax.experimental.pallas import tpu as pltpu
from jax.sharding import PartitionSpec as P

ITERS = 4
AXES = ("gx", "gy", "gz")
LANES = 128
SLOT = 8
SLOTS = 12
SCALARS = 3
NT = (((1,), (1,)), ((), ()))
NN = (((1,), (0,)), ((), ()))
TN = (((0,), (0,)), ((), ()))
f32 = jnp.float32
bf16 = jnp.bfloat16


def own_slot(s):
    return s


COLUMN_OF_FACE = {0: 2, 3: 1, 1: 4, 4: 3}


def whole_lanes(nc):
    return -(-(nc + SCALARS) // 256) * 256


def column_lanes(levels):
    return -(-(30 * levels + SCALARS) // LANES) * LANES


def nbr_slot(s, f):
    if f == 0:
        return 4 + s
    if f == 3:
        return 2 + s
    if f == 1:
        return 8 + s
    if f == 4:
        return 6 + s
    if f == 2:
        return 1 if s == 0 else 11
    return 10 if s == 0 else 0


def split2(x):
    high = x.astype(bf16)
    low = (x - high.astype(f32)).astype(bf16)
    return jnp.concatenate([high, low], 0)


def split3(x):
    high = x.astype(bf16)
    rest = x - high.astype(f32)
    mid = rest.astype(bf16)
    low = (rest - mid.astype(f32)).astype(bf16)
    return jnp.concatenate([high, mid, low], 0)


def fold2(x):
    n = x.shape[0] // 2
    return x[:n] + x[n:]


def fold3(x):
    n = x.shape[0] // 3
    return x[:n] + (x[n : 2 * n] + x[2 * n :])


def mm(a, b, dims):
    return lax.dot_general(a, b, dims, preferred_element_type=f32)


def position(sizes):
    index = [lax.axis_index(a) for a in AXES]
    parity = [lax.rem(i, 2) == 1 for i in index]
    masks = []
    for s in range(2):
        row = []
        for f in range(6):
            d = f % 3
            if d == 2 and (s == 0) == (f == 2):
                row.append(None)
            else:
                inside = (index[d] < sizes[d] - 1) if f < 3 else (index[d] > 0)
                row.append(inside.astype(f32))
        masks.append(row)
    return parity, masks


def masked(value, mask):
    return value if mask is None else value * mask


def pick(cond, a, b):
    return jnp.where(cond, a, b)


def pack_kernel(rhs_in, modes_in, fmap_in, coarse_in, rhs, modes, fmap, coarse, xa, xb, ya, yb, za, zb, sems):
    parity, _ = position((1, 1, 1))
    loads = ((rhs_in, rhs), (modes_in, modes), (fmap_in, fmap), (coarse_in, coarse))
    copies = [pltpu.make_async_copy(source, target, sems.at[k]) for k, (source, target) in enumerate(loads)]
    for copy in copies:
        copy.start()
    for copy in copies:
        copy.wait()
    slabs = -(-coarse.shape[1] // 256)
    for d, outs in ((0, (xa, xb)), (1, (ya, yb))):
        for s in range(2):
            up, down = modes[d, :, s, :], modes[d + 3, :, s, :]
            first = pick(parity[d], down, up)
            second = pick(parity[d], up, down)
            for out, piece in zip(outs, (first, second)):
                out[24 * s : 24 * s + 16, :] = rhs[s, d]
                out[24 * s + 16 : 24 * s + 24, :] = jnp.concatenate(
                    [piece, fmap[d, s : s + 1, :].astype(f32), jnp.zeros((1, 256), f32)], 0
                )
    up, down = modes[2, :, 1, :], modes[5, :, 0, :]
    for out, piece in zip((za, zb), (pick(parity[2], down, up), pick(parity[2], up, down))):
        out[0:16, :] = rhs[1, 2]
        out[16:24, :] = jnp.concatenate([piece, fmap[2, 1:2, :].astype(f32), jnp.zeros((1, 256), f32)], 0)
    for k in range(slabs):
        width = min(256, coarse.shape[1] - 256 * k)
        slab = coarse[:, 256 * k : 256 * k + width]
        if width < 256:
            slab = jnp.concatenate([slab, jnp.zeros((12, 256 - width), f32)], 1)
        gap = jnp.zeros((2, 256), f32)
        slab = jnp.concatenate([slab[:6], gap, slab[6:], gap], 0)
        for out, base in ((xa, 48), (xb, 48), (ya, 48), (yb, 48), (za, 24), (zb, 24)):
            out[base + 16 * k : base + 16 * k + 16, :] = slab


def sides_of(parity, packs):
    plus, minus = [], []
    for d in range(3):
        va, vb = packs[2 * d][...], packs[2 * d + 1][...]
        plus.append(pick(parity[d], vb, va))
        minus.append(pick(parity[d], va, vb))
    return plus, minus


def onehot(row):
    line = lax.broadcasted_iota(jnp.int32, (256, 256), 0)
    return (line == row.astype(jnp.int32)).astype(bf16)


def lower_map(fmap, minus, s, d):
    if d == 2 and s == 1:
        return fmap[2, 0:1, :]
    base = 24 * s if d < 2 else 0
    return minus[d][base + 22 : base + 23, :]


def lower_values(rhs, minus, s, d):
    if d == 2 and s == 1:
        return rhs[0, 2]
    base = 24 * s if d < 2 else 0
    inside = lax.axis_index(AXES[d]) > 0
    return minus[d][base : base + 16, :] * inside.astype(f32)


def begin_kernel(sizes, rhs, modes, fmap, xa, xb, ya, yb, za, zb, touched, part):
    parity, _ = position((1, 1, 1))
    levels = 2 * sizes[2]
    lanes = part.shape[1]
    _, minus = sides_of(parity, (xa, xb, ya, yb, za, zb))
    zero2 = jnp.zeros((2, 256), f32)
    total = jnp.zeros((16, lanes), f32)
    for s in range(2):
        sums = jnp.zeros((48, 16), f32)
        for f in range(6):
            d = f % 3
            if f < 3:
                left = split3(rhs[s, f])
            else:
                table_rows = onehot(lower_map(fmap, minus, s, d))
                left = -mm(split3(lower_values(rhs, minus, s, d)), table_rows, NN)
                left = left.astype(bf16)
            sums += mm(left, split2(jnp.concatenate([modes[f, :, s, :], zero2], 0)), NT)
        own = fold3(sums)
        own = own[:, :8] + own[:, 8:]
        mode = lax.broadcasted_iota(jnp.int32, (8, lanes), 0)
        lane = lax.broadcasted_iota(jnp.int32, (8, lanes), 1)
        level = 2 * lax.axis_index("gz") + s
        choose = ((lane == level * 6 + mode) & (mode < 6)).astype(bf16)
        total += fold3(mm(split3(own), choose, NN))
    part[...] = total


def place_rows(sizes, nc, lanes, width, k):
    gx, gy = lax.axis_index("gx"), lax.axis_index("gy")
    levels = 2 * sizes[2]
    line = lax.broadcasted_iota(jnp.int32, (lanes, 1), 0)
    whole = lax.broadcasted_iota(jnp.int32, (lanes, width), 1)
    y = jnp.bitwise_xor(gy, k)
    aim = jnp.where(line >= 30 * levels, nc + line - 30 * levels, -1)
    for t, (dx, dy) in enumerate(((0, 0), (-1, 0), (1, 0), (0, -1), (0, 1))):
        inside = (gx + dx >= 0) & (gx + dx < sizes[0]) & (y + dy >= 0) & (y + dy < sizes[1])
        first = jnp.where(inside, ((gx + dx) * sizes[1] + y + dy - t) * 6 * levels, -6 * nc)
        aim = jnp.where((line >= t * 6 * levels) & (line < (t + 1) * 6 * levels), line + first, aim)
    return (whole == aim).astype(bf16)


def place_table_kernel(sizes, nc, lanes, place):
    for k in range(sizes[1]):
        place[k * lanes : k * lanes + lanes, :] = place_rows(sizes, nc, lanes, place.shape[1], k)


def touch_kernel(factors, out):
    out[...] = factors[0, 0, 0, 0:16, 0:LANES].astype(f32)[:8]


def turn_kernel(factors, turned):
    for s in range(factors.shape[0]):
        for i in range(factors.shape[1]):
            for j in range(factors.shape[2]):
                turned[s, i, j] = factors[s, i, j].T


def setup_kernel(sizes, rhs, modes, fmap, coarse, xa, xb, ya, yb, za, zb, *refs):
    perm, back, lift, sums, start, solve, work, rows = refs
    parity, _ = position((1, 1, 1))
    nc = coarse.shape[1]
    slabs = -(-nc // 256)
    levels = 2 * sizes[2]
    lanes = column_lanes(levels)
    gz = lax.axis_index("gz")
    plus, minus = sides_of(parity, (xa, xb, ya, yb, za, zb))

    def to_upper_order(values, table_rows):
        return -fold3(mm(split3(values), table_rows, NT))

    zero2 = jnp.zeros((2, 256), f32)
    lane_column = lax.broadcasted_iota(jnp.int32, (16, lanes), 1)
    source_row = lax.broadcasted_iota(jnp.int32, (16, lanes), 0)
    tilde_low = {}
    for s in range(2):
        for d in range(3):
            table_rows = onehot(lower_map(fmap, minus, s, d))
            perm[s * 3 + d] = table_rows
            back[s * 3 + d] = table_rows.T
            tilde_low[s, d] = to_upper_order(modes[d + 3, :, s, :], table_rows)
    work[...] = jnp.zeros(work.shape, f32)
    for s in range(2):
        for f in range(6):
            d = f % 3
            base = 24 * s if d < 2 else 0
            if f < 3:
                own = modes[f, :, s, :]
                start[s, f] = rhs[s, f]
                if d == 2 and s == 0:
                    other = tilde_low[1, 2]
                else:
                    other = to_upper_order(plus[d][base + 16 : base + 22, :], onehot(fmap[d, s : s + 1, :]))
            else:
                own = tilde_low[s, d]
                start[s, f] = lower_values(rhs, minus, s, d)
                other = modes[2, :, 0, :] if d == 2 and s == 1 else minus[d][base + 16 : base + 22, :]
            own = jnp.concatenate([own, zero2], 0)
            other = jnp.concatenate([other, zero2], 0)
            at, n = own_slot(s) * SLOT, nbr_slot(s, f) * SLOT
            work[at : at + 8, :] = own
            work[n : n + 8, :] = other
            lift[s * 6 + f] = split2(work[...])
            work[at : at + 8, :] = jnp.zeros((8, 256), f32)
            work[n : n + 8, :] = jnp.zeros((8, 256), f32)
            pair = split2(jnp.concatenate([own, other], 0))
            level = 2 * gz + s
            if d == 2:
                target = (level + (1 if f == 2 else -1)) * 6
            else:
                target = COLUMN_OF_FACE[f] * 6 * levels + level * 6
            mode = jnp.bitwise_and(source_row, 7)
            aim = jnp.where(source_row < 8, level * 6, target) + mode
            both = ((lane_column == aim) & (mode < 6)).astype(bf16)
            for h in range(2):
                half = pair[16 * h : 16 * h + 16]
                sums[s * 6 + f, :, h * lanes : h * lanes + lanes] = mm(half, both, TN).astype(bf16)

    rows[...] = jnp.zeros(rows.shape, f32)
    pieces = [(2, minus[0], 48, 16), (4, plus[0], 48, 16), (6, minus[1], 48, 16), (8, plus[1], 48, 16)]
    pieces += [(10, minus[2], 24 + 8, 8), (11, plus[2], 24, 8)]
    for k in range(slabs):
        width = min(256, nc - 256 * k)
        slab = coarse[:, 256 * k : 256 * k + width]
        if width < 256:
            slab = jnp.concatenate([slab, jnp.zeros((12, 256 - width), f32)], 1)
        slab = jnp.concatenate([slab[:6], zero2, slab[6:], zero2], 0)
        rows[0:16, 256 * k : 256 * k + 256] = slab
        for slot, source, base, count in pieces:
            rows[slot * SLOT : slot * SLOT + count, 256 * k : 256 * k + 256] = source[
                base + 16 * k : base + 16 * k + count, :
            ]
    solve[...] = split2(rows[...])


def tail(ref, lanes):
    return ref[:, ref.shape[1] - lanes :]


def beside(outs, faces, values):
    if faces:
        for out, face in zip(outs, faces):
            width = face.shape[1]
            out[:, :width] = face[...]
            out[:, width:] = values
    outs[-1][...] = values


def column_kernel(count, *refs):
    lanes = refs[0].shape[1]
    total = refs[0][...]
    for part in refs[1:count]:
        total += tail(part, lanes)
    split = count + (len(refs) - count) // 2
    beside(refs[split:], refs[count:split], total)


def place_kernel(sizes, nc, count, *refs):
    lanes, width = refs[0].shape[1], refs[-1].shape[1]
    lefts = [split3(tail(part, lanes)) for part in refs[:count]]
    faces = (len(refs) - count) // 2
    if (len(refs) - count) % 2:
        total = jnp.zeros((lefts[0].shape[0], width), f32)
        for k, left in enumerate(lefts):
            total += mm(left, place_rows(sizes, nc, lanes, width, k), NN)
        split = count + faces
    else:
        total = mm(jnp.concatenate(lefts, 1), refs[count][...], NN)
        count, split = count + 1, count + faces
    beside(refs[split:], refs[count:split], fold3(total))


def coarse(whole, parts, solve):
    total = whole[...]
    for part in parts:
        total += tail(part, whole.shape[1])
    got = fold3(mm(split3(total[:, : solve.shape[1]]), solve[...], NT))
    return total, got[:, :LANES] + got[:, LANES:]


def lift_left(total):
    left = split3(total)
    return jnp.concatenate([left, left], 1)


def apply_factors(residual, pattern, factors, turned, perm, back, sums, masks, parity, previous, forward, image, sends):
    xa, xb, ya, yb, za, zb, part = sends
    lanes = part.shape[1]
    partial = jnp.zeros((48, 2 * lanes), f32)
    own_sum = jnp.zeros((16, 256), f32)
    square = jnp.zeros((16, 256), f32)
    cross = jnp.zeros((16, 256), f32)
    faces = {}
    for s in range(2):
        sides = []
        for j in range(6):
            value = residual[s][j]
            if j < 3:
                own_sum += value * value
                sides.append(split2(value))
            else:
                sides.append((-mm(split2(value), perm[s * 3 + j - 3], NN)).astype(bf16))
        present = [[pattern[i, s, j].astype(f32).astype(bf16) for j in range(6)] for i in range(6)]
        halves = []
        for i in range(6):
            acc = jnp.zeros((32, 256), f32)
            for j in range(6):
                acc += mm(sides[j] * present[i][j], turned[s, i, j], NN)
            got = fold2(acc)
            forward[s, i] = got
            square += got * got
            if previous is not None:
                cross += got * previous[s][i]
            halves.append(split2(got))
        for j in range(6):
            acc = jnp.zeros((32, 256), f32)
            for i in range(6):
                acc += mm(halves[i] * present[i][j], factors[s, i, j], NN)
            got = fold2(acc)
            if j >= 3:
                got = -fold3(mm(split3(got), back[s * 3 + j - 3], NN))
            got = masked(got, masks[s][j])
            image[s, j] = got
            faces[s, j] = got
            partial += mm(split3(got), sums[s * 6 + j], NN)
    for s in range(2):
        at = slice(256 * s, 256 * s + 256)
        xa[:, at] = pick(parity[0], faces[s, 3], faces[s, 0])
        xb[:, at] = pick(parity[0], faces[s, 0], faces[s, 3])
        ya[:, at] = pick(parity[1], faces[s, 4], faces[s, 1])
        yb[:, at] = pick(parity[1], faces[s, 1], faces[s, 4])
    total = fold3(partial)
    total = total[:, :lanes] + total[:, lanes:]
    lane = lax.broadcasted_iota(jnp.int32, total.shape, 1)
    scalars = 30 * 2 * lax.axis_size("gz")
    for k, values in enumerate((own_sum, square, cross)):
        total = jnp.where(lane == scalars + k, jnp.sum(values, axis=1, keepdims=True), total)
    part[...] = total
    for out, face in ((za, pick(parity[2], faces[0, 5], faces[1, 2])), (zb, pick(parity[2], faces[1, 2], faces[0, 5]))):
        out[:, :256] = face
        out[:, 256:] = total


def first_kernel(sizes, count, pattern, factors, turned, perm, back, lift, sums, solve, start, *refs):
    parity, masks = position(sizes)
    residual, forward, image = refs[count : count + 3]
    left = lift_left(coarse(refs[0], refs[1:count], solve)[1])
    now = [[None] * 6 for _ in range(2)]
    for s in range(2):
        for f in range(6):
            value = start[s, f] - masked(fold3(mm(left, lift[s * 6 + f], NN)), masks[s][f])
            residual[s, f] = value
            now[s][f] = value
    apply_factors(now, pattern, factors, turned, perm, back, sums, masks, parity, None, forward, image, refs[count + 3 :])


def update(sizes, nc, first, faces, parts, state, count):
    parity, masks = position(sizes)
    residual, forward, image, lift, solve, old = state
    total, solution_part = coarse(parts[0], parts[1:], solve)
    left = lift_left(solution_part)
    sums = jnp.sum(total, axis=0, keepdims=True)
    lane = lax.broadcasted_iota(jnp.int32, sums.shape, 1)

    def scalar(k):
        return jnp.sum(jnp.where(lane == nc + k, sums, 0.0), axis=1, keepdims=True)

    rho, curvature = scalar(0), scalar(1)
    if first:
        beta = None
    else:
        direction, moved, along, multipliers, scalars = old
        beta = rho / scalars[0:1, 0:1]
        curvature = curvature + 2.0 * beta * scalar(2) + beta * beta * scalars[1:2, 0:1]
    step = rho / curvature
    out = {}
    for s in range(2):
        for f in range(count):
            d = f % 3
            if d == 2 and (s == 0) == (f == 2):
                other = image[1 - s, 5 if f == 2 else 2]
            else:
                at = 256 * s if d < 2 else 0
                va, vb = (face[:, at : at + 256] for face in faces[2 * d : 2 * d + 2])
                other = pick(parity[d], vb, va) if f < 3 else pick(parity[d], va, vb)
            change = image[s, f] + other - fold3(mm(left, lift[s * 6 + f], NN))
            change = masked(change, masks[s][f])
            value = residual[s, f]
            towards = value
            if not first:
                towards = value + beta * direction[s, f]
                change = change + beta * moved[s, f]
            out[s, f] = (value - step * change, towards, change)
            if f < 3:
                gain = step * towards
                out[s, f] += (gain if first else multipliers[s, f] + gain,)
    return parity, masks, beta, rho, curvature, out


def middle_kernel(sizes, nc, first, count, *refs):
    pattern, factors, turned, perm, back, lift, sums, solve = refs[:8]
    faces, parts = refs[8:14], refs[14 : 14 + count]
    residual, forward, image = refs[14 + count : 17 + count]
    rest = refs[17 + count :]
    if first:
        old = None
    else:
        old, rest = rest[:5], rest[5:]
    new_residual, new_forward, new_image, new_direction, new_moved, new_along, new_multipliers, new_scalars = rest[:8]
    parity, masks, beta, rho, curvature, out = update(
        sizes, nc, first, faces, parts, (residual, forward, image, lift, solve, old), 6
    )
    row = lax.broadcasted_iota(jnp.int32, (8, LANES), 0)
    new_scalars[...] = jnp.where(row == 0, rho, curvature)
    now = [[None] * 6 for _ in range(2)]
    along = [[None] * 6 for _ in range(2)]
    for s in range(2):
        for f in range(6):
            values = out[s, f]
            now[s][f] = values[0]
            new_residual[s, f] = values[0]
            new_direction[s, f] = values[1]
            new_moved[s, f] = values[2]
            if f < 3:
                new_multipliers[s, f] = values[3]
            line = forward[s, f] if first else forward[s, f] + beta * old[2][s, f]
            along[s][f] = line
            new_along[s, f] = line
    apply_factors(now, pattern, factors, turned, perm, back, sums, masks, parity, along, new_forward, new_image, rest[8:])


def last_kernel(sizes, nc, count, lift, solve, *refs):
    faces, parts = refs[:6], refs[6 : 6 + count]
    residual, forward, image = refs[6 + count : 9 + count]
    old = refs[9 + count : 14 + count]
    multipliers, final = refs[14 + count :]
    out = update(sizes, nc, False, faces, parts, (residual, forward, image, lift, solve, old), 3)[5]
    for s in range(2):
        for f in range(3):
            final[s, f] = out[s, f][0]
            multipliers[s, f] = out[s, f][3]


def swap(values, axis, distance):
    return lax.ppermute(values, axis, [(i, i ^ distance) for i in range(lax.axis_size(axis))])


def exchange(first, second, axis, alone=None, ends=True):
    size = lax.axis_size(axis)
    below = swap(first, axis, 1)
    if size == 2:
        return below, below, [below]
    pairs = [(i, i + 1 if i % 2 else i - 1) for i in range(size)]
    if ends:
        pairs = [(i, j % size) for i, j in pairs]
    else:
        pairs = [(i, j) for i, j in pairs if 0 <= j < size]
    above = lax.ppermute(second, axis, pairs)
    others = [below]
    if alone is not None:
        for distance in range(2, size):
            others.append(above if size == 4 and distance == 3 else swap(alone, axis, distance))
    return below, above, others


def per_device(dual_rhs, factors, block_pattern, face_map, rigid_modes, coarse_solve):
    sizes = tuple(lax.axis_size(a) for a in AXES)
    cases, dofs = dual_rhs.shape[4:]
    nc = coarse_solve.shape[1]
    slabs = -(-nc // 256)
    rhs = dual_rhs.reshape(dual_rhs.shape[2:])
    factors = factors.reshape(factors.shape[2:])
    pattern = block_pattern.reshape(block_pattern.shape[2:]).transpose(1, 0, 2)
    fmap = face_map.reshape(face_map.shape[2:]).transpose(1, 0, 2)
    modes = rigid_modes.reshape(rigid_modes.shape[2:]).transpose(1, 2, 0, 3)
    vmem = pl.BlockSpec(memory_space=pltpu.VMEM)
    smem = pl.BlockSpec(memory_space=pltpu.SMEM)
    params = pltpu.CompilerParams(vmem_limit_bytes=24 << 20)

    def shape(*dims, dtype=f32):
        return jax.ShapeDtypeStruct(dims, dtype)

    anywhere = pl.BlockSpec(memory_space=pl.ANY)

    def call(kernel, outs, ins, specs=None, scratch=(), cost=None):
        specs = specs or {}
        return pl.pallas_call(
            kernel,
            out_shape=outs,
            in_specs=[specs.get(i, vmem) for i in range(len(ins))],
            out_specs=[vmem] * len(outs),
            scratch_shapes=list(scratch),
            compiler_params=params,
            cost_estimate=cost,
        )(*ins)

    levels = 2 * sizes[2]
    lanes, whole = column_lanes(levels), whole_lanes(nc)
    packs = [shape(48 + 16 * slabs, dofs)] * 4 + [shape(24 + 16 * slabs, dofs)] * 2
    raw = [rhs, modes, fmap, coarse_solve]
    rhs, modes, fmap, coarse_rows, xa, xb, ya, yb, za, zb = call(
        pack_kernel,
        [jax.ShapeDtypeStruct(x.shape, x.dtype) for x in raw] + packs,
        raw,
        specs={i: anywhere for i in range(4)},
        scratch=(pltpu.SemaphoreType.DMA((4,)),),
    )
    place = []
    if sizes[1] * lanes * whole <= 1 << 20:
        place = call(
            functools.partial(place_table_kernel, sizes, nc, lanes),
            [shape(sizes[1] * lanes, whole, dtype=bf16)],
            [],
            cost=pl.CostEstimate(flops=0, bytes_accessed=4 << 20, transcendentals=0),
        )
    za, zb, _ = exchange(za, zb, "gz", ends=False)
    xa, xb, _ = exchange(xa, xb, "gx", ends=False)
    ya, yb, _ = exchange(ya, yb, "gy", ends=False)
    packs = [xa, xb, ya, yb, za, zb]
    (turned,) = call(
        turn_kernel,
        [jax.ShapeDtypeStruct(factors.shape, factors.dtype)],
        [factors],
        cost=pl.CostEstimate(flops=0, bytes_accessed=9 << 20, transcendentals=0),
    )
    faces = shape(2, 6, cases, dofs)
    (touched,) = call(
        touch_kernel,
        [shape(8, LANES)],
        [factors],
        cost=pl.CostEstimate(flops=0, bytes_accessed=9 << 20, transcendentals=0),
    )
    (part,) = call(functools.partial(begin_kernel, sizes), [shape(cases, lanes)], [rhs, modes, fmap, *packs, touched])
    perm, back, lift, sums, start, solve = call(
        functools.partial(setup_kernel, sizes),
        [
            shape(6, dofs, dofs, dtype=bf16),
            shape(6, dofs, dofs, dtype=bf16),
            shape(12, 2 * LANES, dofs, dtype=bf16),
            shape(12, dofs, 2 * lanes, dtype=bf16),
            faces,
            shape(2 * LANES, 256 * slabs, dtype=bf16),
        ],
        [rhs, modes, fmap, coarse_rows, *packs],
        scratch=(pltpu.VMEM((LANES, dofs), f32), pltpu.VMEM((LANES, 256 * slabs), f32)),
        cost=pl.CostEstimate(flops=0, bytes_accessed=9 << 20, transcendentals=0),
    )

    def reduce(part, za, zb, along_y, along_x, also=None):
        za, zb, others = exchange(za, zb, "gz", part)
        outs = [shape(cases, face.shape[1] + lanes) for face in along_y] + [shape(cases, lanes)]
        ins = [part, *others, *along_y]
        *along_y, part = call(functools.partial(column_kernel, 1 + len(others)), outs, ins)
        ya, yb, others = exchange(*(along_y or (part, part)), "gy", part)
        outs = [shape(cases, face.shape[1] + whole) for face in along_x] + [shape(cases, whole)]
        if also is not None:
            part, also = lax.optimization_barrier((part, also))
        ins = [part, *others, *place, *along_x]
        *along_x, part = call(functools.partial(place_kernel, sizes, nc, 1 + len(others)), outs, ins)
        xa, xb, others = exchange(*(along_x or (part, part)), "gx", part)
        return [xa, xb, ya, yb, za, zb], [part, *others], also

    _, parts, turned = reduce(part, part, part, (), (), turned)
    wide = shape(cases, 2 * dofs)
    sends = [wide] * 4 + [shape(cases, dofs + lanes)] * 2 + [shape(cases, lanes)]
    residual, forward, image, *out = call(
        functools.partial(first_kernel, sizes, len(parts)),
        [faces, faces, faces] + sends,
        [pattern, factors, turned, perm, back, lift, sums, solve, start, *parts],
        specs={0: smem},
    )
    old = []
    for iteration in range(ITERS - 1):
        xa, xb, ya, yb, za, zb, part = out
        got, parts, _ = reduce(part, za, zb, (ya, yb), (xa, xb))
        residual, forward, image, *out = call(
            functools.partial(middle_kernel, sizes, nc, iteration == 0, len(parts)),
            [faces] * 6 + [shape(2, 3, cases, dofs), shape(8, LANES)] + sends,
            [pattern, factors, turned, perm, back, lift, sums, solve, *got, *parts, residual, forward, image, *old],
            specs={0: smem},
        )
        old, out = out[:5], out[5:]
    xa, xb, ya, yb, za, zb, part = out
    got, parts, _ = reduce(part, za, zb, (ya, yb), (xa, xb))
    multipliers, final = call(
        functools.partial(last_kernel, sizes, nc, len(parts)),
        [shape(2, 3, cases, dofs)] * 2,
        [lift, solve, *got, *parts, residual, forward, image, *old],
    )
    return multipliers.reshape(dual_rhs.shape), final.reshape(dual_rhs.shape)


def solution(mesh):
    return jax.shard_map(
        per_device,
        mesh=mesh,
        in_specs=(
            P("gx", "gy", "gz", None, None, None),
            P("gx", "gy", "gz", None, None, None, None),
            P("gx", "gy", "gz", None, None),
            P("gx", "gy", "gz", None, None),
            P("gx", "gy", "gz", None, None, None),
            P(("gx", "gy", "gz"), None),
        ),
        out_specs=(P("gx", "gy", "gz", None, None, None), P("gx", "gy", "gz", None, None, None)),
        check_vma=False,
    )
```

```python
import functools

import jax
import jax.numpy as jnp
from jax import lax
from jax.experimental import pallas as pl
from jax.experimental.pallas import tpu as pltpu
from jax.sharding import PartitionSpec as P

ITERS = 4
AXES = ("gx", "gy", "gz")
LANES = 128
SLOT = 8
SLOTS = 12
SCALARS = 3
NT = (((1,), (1,)), ((), ()))
NN = (((1,), (0,)), ((), ()))
TN = (((0,), (0,)), ((), ()))
f32 = jnp.float32
bf16 = jnp.bfloat16


def own_slot(s):
    return s


COLUMN_OF_FACE = {0: 2, 3: 1, 1: 4, 4: 3}


def whole_lanes(nc):
    return -(-(nc + SCALARS) // 256) * 256


def column_lanes(levels):
    return -(-(30 * levels + SCALARS) // LANES) * LANES


def nbr_slot(s, f):
    if f == 0:
        return 4 + s
    if f == 3:
        return 2 + s
    if f == 1:
        return 8 + s
    if f == 4:
        return 6 + s
    if f == 2:
        return 1 if s == 0 else 11
    return 10 if s == 0 else 0


def split2(x):
    high = x.astype(bf16)
    low = (x - high.astype(f32)).astype(bf16)
    return jnp.concatenate([high, low], 0)


def split3(x):
    high = x.astype(bf16)
    rest = x - high.astype(f32)
    mid = rest.astype(bf16)
    low = (rest - mid.astype(f32)).astype(bf16)
    return jnp.concatenate([high, mid, low], 0)


def fold2(x):
    n = x.shape[0] // 2
    return x[:n] + x[n:]


def fold3(x):
    n = x.shape[0] // 3
    return x[:n] + (x[n : 2 * n] + x[2 * n :])


def mm(a, b, dims):
    return lax.dot_general(a, b, dims, preferred_element_type=f32)


def position(sizes):
    index = [lax.axis_index(a) for a in AXES]
    parity = [lax.rem(i, 2) == 1 for i in index]
    masks = []
    for s in range(2):
        row = []
        for f in range(6):
            d = f % 3
            if d == 2 and (s == 0) == (f == 2):
                row.append(None)
            else:
                inside = (index[d] < sizes[d] - 1) if f < 3 else (index[d] > 0)
                row.append(inside.astype(f32))
        masks.append(row)
    return parity, masks


def masked(value, mask):
    return value if mask is None else value * mask


def pick(cond, a, b):
    return jnp.where(cond, a, b)


def pack_kernel(rhs_in, modes_in, fmap_in, coarse_in, rhs, modes, fmap, coarse, xa, xb, ya, yb, za, zb, sems):
    parity, _ = position((1, 1, 1))
    loads = ((rhs_in, rhs), (modes_in, modes), (fmap_in, fmap), (coarse_in, coarse))
    copies = [pltpu.make_async_copy(source, target, sems.at[k]) for k, (source, target) in enumerate(loads)]
    for copy in copies:
        copy.start()
    for copy in copies:
        copy.wait()
    slabs = -(-coarse.shape[1] // 256)
    for d, outs in ((0, (xa, xb)), (1, (ya, yb))):
        for s in range(2):
            up, down = modes[d, :, s, :], modes[d + 3, :, s, :]
            first = pick(parity[d], down, up)
            second = pick(parity[d], up, down)
            for out, piece in zip(outs, (first, second)):
                out[24 * s : 24 * s + 16, :] = rhs[s, d]
                out[24 * s + 16 : 24 * s + 24, :] = jnp.concatenate(
                    [piece, fmap[d, s : s + 1, :].astype(f32), jnp.zeros((1, 256), f32)], 0
                )
    up, down = modes[2, :, 1, :], modes[5, :, 0, :]
    for out, piece in zip((za, zb), (pick(parity[2], down, up), pick(parity[2], up, down))):
        out[0:16, :] = rhs[1, 2]
        out[16:24, :] = jnp.concatenate([piece, fmap[2, 1:2, :].astype(f32), jnp.zeros((1, 256), f32)], 0)
    for k in range(slabs):
        width = min(256, coarse.shape[1] - 256 * k)
        slab = coarse[:, 256 * k : 256 * k + width]
        if width < 256:
            slab = jnp.concatenate([slab, jnp.zeros((12, 256 - width), f32)], 1)
        gap = jnp.zeros((2, 256), f32)
        slab = jnp.concatenate([slab[:6], gap, slab[6:], gap], 0)
        for out, base in ((xa, 48), (xb, 48), (ya, 48), (yb, 48), (za, 24), (zb, 24)):
            out[base + 16 * k : base + 16 * k + 16, :] = slab


def sides_of(parity, packs):
    plus, minus = [], []
    for d in range(3):
        va, vb = packs[2 * d][...], packs[2 * d + 1][...]
        plus.append(pick(parity[d], vb, va))
        minus.append(pick(parity[d], va, vb))
    return plus, minus


def onehot(row):
    line = lax.broadcasted_iota(jnp.int32, (256, 256), 0)
    return (line == row.astype(jnp.int32)).astype(bf16)


def lower_map(fmap, minus, s, d):
    if d == 2 and s == 1:
        return fmap[2, 0:1, :]
    base = 24 * s if d < 2 else 0
    return minus[d][base + 22 : base + 23, :]


def lower_values(rhs, minus, s, d):
    if d == 2 and s == 1:
        return rhs[0, 2]
    base = 24 * s if d < 2 else 0
    inside = lax.axis_index(AXES[d]) > 0
    return minus[d][base : base + 16, :] * inside.astype(f32)


def begin_kernel(sizes, rhs, modes, fmap, xa, xb, ya, yb, za, zb, touched, part):
    parity, _ = position((1, 1, 1))
    levels = 2 * sizes[2]
    lanes = part.shape[1]
    _, minus = sides_of(parity, (xa, xb, ya, yb, za, zb))
    zero2 = jnp.zeros((2, 256), f32)
    total = jnp.zeros((16, lanes), f32)
    for s in range(2):
        sums = jnp.zeros((48, 16), f32)
        for f in range(6):
            d = f % 3
            if f < 3:
                left = split3(rhs[s, f])
            else:
                table_rows = onehot(lower_map(fmap, minus, s, d))
                left = -mm(split3(lower_values(rhs, minus, s, d)), table_rows, NN)
                left = left.astype(bf16)
            sums += mm(left, split2(jnp.concatenate([modes[f, :, s, :], zero2], 0)), NT)
        own = fold3(sums)
        own = own[:, :8] + own[:, 8:]
        mode = lax.broadcasted_iota(jnp.int32, (8, lanes), 0)
        lane = lax.broadcasted_iota(jnp.int32, (8, lanes), 1)
        level = 2 * lax.axis_index("gz") + s
        choose = ((lane == level * 6 + mode) & (mode < 6)).astype(bf16)
        total += fold3(mm(split3(own), choose, NN))
    part[...] = total


def place_rows(sizes, nc, lanes, width, k):
    gx, gy = lax.axis_index("gx"), lax.axis_index("gy")
    levels = 2 * sizes[2]
    line = lax.broadcasted_iota(jnp.int32, (lanes, 1), 0)
    whole = lax.broadcasted_iota(jnp.int32, (lanes, width), 1)
    y = jnp.bitwise_xor(gy, k)
    aim = jnp.where(line >= 30 * levels, nc + line - 30 * levels, -1)
    for t, (dx, dy) in enumerate(((0, 0), (-1, 0), (1, 0), (0, -1), (0, 1))):
        inside = (gx + dx >= 0) & (gx + dx < sizes[0]) & (y + dy >= 0) & (y + dy < sizes[1])
        first = jnp.where(inside, ((gx + dx) * sizes[1] + y + dy - t) * 6 * levels, -6 * nc)
        aim = jnp.where((line >= t * 6 * levels) & (line < (t + 1) * 6 * levels), line + first, aim)
    return (whole == aim).astype(bf16)


def place_table_kernel(sizes, nc, lanes, place):
    for k in range(sizes[1]):
        place[k * lanes : k * lanes + lanes, :] = place_rows(sizes, nc, lanes, place.shape[1], k)


def touch_kernel(factors, out):
    out[...] = factors[0, 0, 0, 0:16, 0:LANES].astype(f32)[:8]


def turn_kernel(factors, turned):
    for s in range(factors.shape[0]):
        for i in range(factors.shape[1]):
            for j in range(factors.shape[2]):
                turned[s, i, j] = factors[s, i, j].T


def setup_kernel(sizes, rhs, modes, fmap, coarse, xa, xb, ya, yb, za, zb, *refs):
    perm, back, lift, sums, start, solve, pairs, work, rows = refs
    parity, _ = position((1, 1, 1))
    nc = coarse.shape[1]
    slabs = -(-nc // 256)
    levels = 2 * sizes[2]
    lanes = column_lanes(levels)
    gz = lax.axis_index("gz")
    plus, minus = sides_of(parity, (xa, xb, ya, yb, za, zb))

    def to_upper_order(values, table_rows):
        return -fold3(mm(split3(values), table_rows, NT))

    zero2 = jnp.zeros((2, 256), f32)
    lane_column = lax.broadcasted_iota(jnp.int32, (16, lanes), 1)
    source_row = lax.broadcasted_iota(jnp.int32, (16, lanes), 0)
    tilde_low = {}
    for s in range(2):
        for d in range(3):
            table_rows = onehot(lower_map(fmap, minus, s, d))
            perm[s * 3 + d] = table_rows
            back[s * 3 + d] = table_rows.T
            tilde_low[s, d] = to_upper_order(modes[d + 3, :, s, :], table_rows)
    work[...] = jnp.zeros(work.shape, f32)
    for s in range(2):
        for f in range(6):
            d = f % 3
            base = 24 * s if d < 2 else 0
            if f < 3:
                own = modes[f, :, s, :]
                start[s, f] = rhs[s, f]
                if d == 2 and s == 0:
                    other = tilde_low[1, 2]
                else:
                    other = to_upper_order(plus[d][base + 16 : base + 22, :], onehot(fmap[d, s : s + 1, :]))
            else:
                own = tilde_low[s, d]
                start[s, f] = lower_values(rhs, minus, s, d)
                other = modes[2, :, 0, :] if d == 2 and s == 1 else minus[d][base + 16 : base + 22, :]
            own = jnp.concatenate([own, zero2], 0)
            other = jnp.concatenate([other, zero2], 0)
            at, n = own_slot(s) * SLOT, nbr_slot(s, f) * SLOT
            work[at : at + 8, :] = own
            work[n : n + 8, :] = other
            lift[s * 6 + f] = split2(work[...])
            work[at : at + 8, :] = jnp.zeros((8, 256), f32)
            work[n : n + 8, :] = jnp.zeros((8, 256), f32)
            pair = split2(jnp.concatenate([own, other], 0))
            pairs[s * 6 + f] = pair
            level = 2 * gz + s
            if d == 2:
                target = (level + (1 if f == 2 else -1)) * 6
            else:
                target = COLUMN_OF_FACE[f] * 6 * levels + level * 6
            mode = jnp.bitwise_and(source_row, 7)
            aim = jnp.where(source_row < 8, level * 6, target) + mode
            both = ((lane_column == aim) & (mode < 6)).astype(bf16)
            for h in range(2):
                half = pair[16 * h : 16 * h + 16]
                sums[s * 6 + f, :, h * lanes : h * lanes + lanes] = mm(half, both, TN).astype(bf16)

    rows[...] = jnp.zeros(rows.shape, f32)
    pieces = [(2, minus[0], 48, 16), (4, plus[0], 48, 16), (6, minus[1], 48, 16), (8, plus[1], 48, 16)]
    pieces += [(10, minus[2], 24 + 8, 8), (11, plus[2], 24, 8)]
    for k in range(slabs):
        width = min(256, nc - 256 * k)
        slab = coarse[:, 256 * k : 256 * k + width]
        if width < 256:
            slab = jnp.concatenate([slab, jnp.zeros((12, 256 - width), f32)], 1)
        slab = jnp.concatenate([slab[:6], zero2, slab[6:], zero2], 0)
        rows[0:16, 256 * k : 256 * k + 256] = slab
        for slot, source, base, count in pieces:
            rows[slot * SLOT : slot * SLOT + count, 256 * k : 256 * k + 256] = source[
                base + 16 * k : base + 16 * k + count, :
            ]
    solve[...] = split2(rows[...])


def tail(ref, lanes):
    return ref[:, ref.shape[1] - lanes :]


def beside(outs, faces, values):
    if faces:
        for out, face in zip(outs, faces):
            width = face.shape[1]
            out[:, :width] = face[...]
            out[:, width:] = values
    outs[-1][...] = values


def column_kernel(count, *refs):
    lanes = refs[0].shape[1]
    total = refs[0][...]
    for part in refs[1:count]:
        total += tail(part, lanes)
    split = count + (len(refs) - count) // 2
    beside(refs[split:], refs[count:split], total)


def place_kernel(sizes, nc, count, *refs):
    lanes, width = refs[0].shape[1], refs[-1].shape[1]
    lefts = [split3(tail(part, lanes)) for part in refs[:count]]
    faces = (len(refs) - count) // 2
    if (len(refs) - count) % 2:
        total = jnp.zeros((lefts[0].shape[0], width), f32)
        for k, left in enumerate(lefts):
            total += mm(left, place_rows(sizes, nc, lanes, width, k), NN)
        split = count + faces
    else:
        total = mm(jnp.concatenate(lefts, 1), refs[count][...], NN)
        count, split = count + 1, count + faces
    beside(refs[split:], refs[count:split], fold3(total))


def coarse(whole, parts, solve):
    total = whole[...]
    for part in parts:
        total += tail(part, whole.shape[1])
    got = fold3(mm(split3(total[:, : solve.shape[1]]), solve[...], NT))
    return total, got[:, :LANES] + got[:, LANES:]


def lift_left(total):
    left = split3(total)
    return jnp.concatenate([left, left], 1)


def forward_faces(faces, js, pattern, turned, perm):
    sums = {}
    for s in range(2):
        sides = {}
        for j in js:
            rows = faces[s, j]
            sides[j] = rows if j < 3 else (-mm(rows, perm[s * 3 + j - 3], NN)).astype(bf16)
        for i in range(6):
            acc = jnp.zeros((32, 256), f32)
            for j in js:
                acc += mm(sides[j] * pattern[i, s, j].astype(f32).astype(bf16), turned[s, i, j], NN)
            sums[s, i] = acc
    return sums


def lifted_kernel(sizes, pattern, turned, perm, pairs, out, work):
    _, masks = position(sizes)
    for s in range(2):
        for i in range(6):
            work[s * 6 + i] = jnp.zeros((LANES, 256), f32)
    for j in range(6):
        faces = {}
        for s in range(2):
            rows = pairs[s * 6 + j]
            faces[s, j] = rows if masks[s][j] is None else (rows.astype(f32) * masks[s][j]).astype(bf16)
        sums = forward_faces(faces, (j,), pattern, turned, perm)
        for s in range(2):
            at, n = own_slot(s) * SLOT, nbr_slot(s, j) * SLOT
            for i in range(6):
                got = fold2(sums[s, i])
                work[s * 6 + i, at : at + 8, :] += got[:8]
                work[s * 6 + i, n : n + 8, :] += got[8:]
    for k in range(12):
        out[k] = split2(work[k])


def sum_of_sides(s, f, image, pair, parity, mask):
    d = f % 3
    if pair is None:
        other = image[1 - s, 5 if f == 2 else 2]
    else:
        at = 256 * s if d < 2 else 0
        va, vb = (face[:, at : at + 256] for face in pair)
        other = pick(parity[d], vb, va) if f < 3 else pick(parity[d], va, vb)
    return masked(image[s, f] + other, mask)


def early_kernel(sizes, pattern, turned, perm, image, ya, yb, za, zb, out):
    parity, masks = position(sizes)
    faces = {}
    for s in range(2):
        for f in (1, 2, 4, 5):
            inner = f % 3 == 2 and (s == 0) == (f == 2)
            pair = None if inner else (ya, yb) if f % 3 == 1 else (za, zb)
            faces[s, f] = split2(sum_of_sides(s, f, image, pair, parity, masks[s][f]))
    sums = forward_faces(faces, (1, 2, 4, 5), pattern, turned, perm)
    for s in range(2):
        for i in range(6):
            out[s, i] = fold2(sums[s, i])


def apply_factors(residual, pattern, factors, turned, perm, back, sums, masks, parity, previous, forward, image, sends, given=None):
    xa, xb, ya, yb, za, zb, part = sends
    lanes = part.shape[1]
    partial = jnp.zeros((48, 2 * lanes), f32)
    own_sum = jnp.zeros((16, 256), f32)
    square = jnp.zeros((16, 256), f32)
    cross = jnp.zeros((16, 256), f32)
    faces = {}
    for s in range(2):
        sides = []
        for j in range(6):
            value = residual[s][j]
            if j < 3:
                own_sum += value * value
                sides.append(split2(value))
            elif given is None:
                sides.append((-mm(split2(value), perm[s * 3 + j - 3], NN)).astype(bf16))
        present = [[pattern[i, s, j].astype(f32).astype(bf16) for j in range(6)] for i in range(6)]
        halves = []
        for i in range(6):
            if given is None:
                acc = jnp.zeros((32, 256), f32)
                for j in range(6):
                    acc += mm(sides[j] * present[i][j], turned[s, i, j], NN)
                got = fold2(acc)
            else:
                got = given[s, i]
            forward[s, i] = got
            square += got * got
            if previous is not None:
                cross += got * previous[s][i]
            halves.append(split2(got))
        for j in range(6):
            acc = jnp.zeros((32, 256), f32)
            for i in range(6):
                acc += mm(halves[i] * present[i][j], factors[s, i, j], NN)
            got = fold2(acc)
            if j >= 3:
                got = -fold3(mm(split3(got), back[s * 3 + j - 3], NN))
            got = masked(got, masks[s][j])
            image[s, j] = got
            faces[s, j] = got
            partial += mm(split3(got), sums[s * 6 + j], NN)
    for s in range(2):
        at = slice(256 * s, 256 * s + 256)
        xa[:, at] = pick(parity[0], faces[s, 3], faces[s, 0])
        xb[:, at] = pick(parity[0], faces[s, 0], faces[s, 3])
        ya[:, at] = pick(parity[1], faces[s, 4], faces[s, 1])
        yb[:, at] = pick(parity[1], faces[s, 1], faces[s, 4])
    total = fold3(partial)
    total = total[:, :lanes] + total[:, lanes:]
    lane = lax.broadcasted_iota(jnp.int32, total.shape, 1)
    scalars = 30 * 2 * lax.axis_size("gz")
    for k, values in enumerate((own_sum, square, cross)):
        total = jnp.where(lane == scalars + k, jnp.sum(values, axis=1, keepdims=True), total)
    part[...] = total
    for out, face in ((za, pick(parity[2], faces[0, 5], faces[1, 2])), (zb, pick(parity[2], faces[1, 2], faces[0, 5]))):
        out[:, :256] = face
        out[:, 256:] = total


def first_kernel(sizes, count, pattern, factors, turned, perm, back, lift, sums, solve, start, *refs):
    parity, masks = position(sizes)
    residual, forward, image = refs[count : count + 3]
    left = lift_left(coarse(refs[0], refs[1:count], solve)[1])
    now = [[None] * 6 for _ in range(2)]
    for s in range(2):
        for f in range(6):
            value = start[s, f] - masked(fold3(mm(left, lift[s * 6 + f], NN)), masks[s][f])
            residual[s, f] = value
            now[s][f] = value
    apply_factors(now, pattern, factors, turned, perm, back, sums, masks, parity, None, forward, image, refs[count + 3 :])


def update(sizes, nc, first, faces, parts, state, count):
    parity, masks = position(sizes)
    residual, forward, image, lift, solve, old = state
    total, solution_part = coarse(parts[0], parts[1:], solve)
    left = lift_left(solution_part)
    sums = jnp.sum(total, axis=0, keepdims=True)
    lane = lax.broadcasted_iota(jnp.int32, sums.shape, 1)

    def scalar(k):
        return jnp.sum(jnp.where(lane == nc + k, sums, 0.0), axis=1, keepdims=True)

    rho, curvature = scalar(0), scalar(1)
    if first:
        beta = None
    else:
        direction, moved, along, multipliers, scalars = old[:5]
        beta = rho / scalars[0:1, 0:1]
        curvature = curvature + 2.0 * beta * scalar(2) + beta * beta * scalars[1:2, 0:1]
    step = rho / curvature
    out, jumps = {}, {}
    for s in range(2):
        for f in range(count):
            d = f % 3
            inner = d == 2 and (s == 0) == (f == 2)
            pair = None if inner else faces[2 * d : 2 * d + 2]
            change = sum_of_sides(s, f, image, pair, parity, masks[s][f])
            if d == 0:
                jumps[s, f] = split2(change)
            change -= masked(fold3(mm(left, lift[s * 6 + f], NN)), masks[s][f])
            value = residual[s, f]
            towards = value
            if not first:
                towards = value + beta * direction[s, f]
                change = change + beta * moved[s, f]
            out[s, f] = (value - step * change, towards, change)
            if f < 3:
                gain = step * towards
                out[s, f] += (gain if first else multipliers[s, f] + gain,)
    return parity, masks, beta, rho, curvature, out, left, step, jumps


def middle_kernel(sizes, nc, first, count, *refs):
    pattern, factors, turned, perm, back, lift, sums, solve, lifted, early = refs[:10]
    faces, parts = refs[10:16], refs[16 : 16 + count]
    residual, forward, image = refs[16 + count : 19 + count]
    rest = refs[19 + count :]
    if first:
        old = None
    else:
        old, rest = rest[:6], rest[6:]
    new_residual, new_forward, new_image, new_direction, new_moved, new_along, new_multipliers, new_scalars = rest[:8]
    new_pushed = rest[8]
    parity, masks, beta, rho, curvature, out, left, step, jumps = update(
        sizes, nc, first, faces, parts, (residual, forward, image, lift, solve, old), 6
    )
    sides = forward_faces(jumps, (0, 3), pattern, turned, perm)
    given = {}
    for s in range(2):
        for i in range(6):
            pushed = early[s, i] + fold2(sides[s, i]) - fold3(mm(left, lifted[s * 6 + i], NN))
            if not first:
                pushed += beta * old[5][s, i]
            new_pushed[s, i] = pushed
            given[s, i] = forward[s, i] - step * pushed
    row = lax.broadcasted_iota(jnp.int32, (8, LANES), 0)
    new_scalars[...] = jnp.where(row == 0, rho, curvature)
    now = [[None] * 6 for _ in range(2)]
    along = [[None] * 6 for _ in range(2)]
    for s in range(2):
        for f in range(6):
            values = out[s, f]
            now[s][f] = values[0]
            new_residual[s, f] = values[0]
            new_direction[s, f] = values[1]
            new_moved[s, f] = values[2]
            if f < 3:
                new_multipliers[s, f] = values[3]
            line = forward[s, f] if first else forward[s, f] + beta * old[2][s, f]
            along[s][f] = line
            new_along[s, f] = line
    apply_factors(now, pattern, factors, turned, perm, back, sums, masks, parity, along, new_forward, new_image, rest[9:], given)


def last_kernel(sizes, nc, count, lift, solve, *refs):
    faces, parts = refs[:6], refs[6 : 6 + count]
    residual, forward, image = refs[6 + count : 9 + count]
    old = refs[9 + count : 14 + count]
    multipliers, final = refs[14 + count :]
    out = update(sizes, nc, False, faces, parts, (residual, forward, image, lift, solve, old), 3)[5]
    for s in range(2):
        for f in range(3):
            final[s, f] = out[s, f][0]
            multipliers[s, f] = out[s, f][3]


def swap(values, axis, distance):
    return lax.ppermute(values, axis, [(i, i ^ distance) for i in range(lax.axis_size(axis))])


def exchange(first, second, axis, alone=None, ends=True):
    size = lax.axis_size(axis)
    below = swap(first, axis, 1)
    if size == 2:
        return below, below, [below]
    pairs = [(i, i + 1 if i % 2 else i - 1) for i in range(size)]
    if ends:
        pairs = [(i, j % size) for i, j in pairs]
    else:
        pairs = [(i, j) for i, j in pairs if 0 <= j < size]
    above = lax.ppermute(second, axis, pairs)
    others = [below]
    if alone is not None:
        for distance in range(2, size):
            others.append(above if size == 4 and distance == 3 else swap(alone, axis, distance))
    return below, above, others


def per_device(dual_rhs, factors, block_pattern, face_map, rigid_modes, coarse_solve):
    sizes = tuple(lax.axis_size(a) for a in AXES)
    cases, dofs = dual_rhs.shape[4:]
    nc = coarse_solve.shape[1]
    slabs = -(-nc // 256)
    rhs = dual_rhs.reshape(dual_rhs.shape[2:])
    factors = factors.reshape(factors.shape[2:])
    pattern = block_pattern.reshape(block_pattern.shape[2:]).transpose(1, 0, 2)
    fmap = face_map.reshape(face_map.shape[2:]).transpose(1, 0, 2)
    modes = rigid_modes.reshape(rigid_modes.shape[2:]).transpose(1, 2, 0, 3)
    vmem = pl.BlockSpec(memory_space=pltpu.VMEM)
    smem = pl.BlockSpec(memory_space=pltpu.SMEM)
    params = pltpu.CompilerParams(vmem_limit_bytes=24 << 20)

    def shape(*dims, dtype=f32):
        return jax.ShapeDtypeStruct(dims, dtype)

    anywhere = pl.BlockSpec(memory_space=pl.ANY)

    def call(kernel, outs, ins, specs=None, scratch=(), cost=None):
        specs = specs or {}
        return pl.pallas_call(
            kernel,
            out_shape=outs,
            in_specs=[specs.get(i, vmem) for i in range(len(ins))],
            out_specs=[vmem] * len(outs),
            scratch_shapes=list(scratch),
            compiler_params=params,
            cost_estimate=cost,
        )(*ins)

    levels = 2 * sizes[2]
    lanes, whole = column_lanes(levels), whole_lanes(nc)
    packs = [shape(48 + 16 * slabs, dofs)] * 4 + [shape(24 + 16 * slabs, dofs)] * 2
    raw = [rhs, modes, fmap, coarse_solve]
    rhs, modes, fmap, coarse_rows, xa, xb, ya, yb, za, zb = call(
        pack_kernel,
        [jax.ShapeDtypeStruct(x.shape, x.dtype) for x in raw] + packs,
        raw,
        specs={i: anywhere for i in range(4)},
        scratch=(pltpu.SemaphoreType.DMA((4,)),),
    )
    place = []
    if sizes[1] * lanes * whole <= 1 << 20:
        place = call(
            functools.partial(place_table_kernel, sizes, nc, lanes),
            [shape(sizes[1] * lanes, whole, dtype=bf16)],
            [],
            cost=pl.CostEstimate(flops=0, bytes_accessed=4 << 20, transcendentals=0),
        )
    za, zb, _ = exchange(za, zb, "gz", ends=False)
    xa, xb, _ = exchange(xa, xb, "gx", ends=False)
    ya, yb, _ = exchange(ya, yb, "gy", ends=False)
    packs = [xa, xb, ya, yb, za, zb]
    (turned,) = call(
        turn_kernel,
        [jax.ShapeDtypeStruct(factors.shape, factors.dtype)],
        [factors],
        cost=pl.CostEstimate(flops=0, bytes_accessed=9 << 20, transcendentals=0),
    )
    faces = shape(2, 6, cases, dofs)
    (touched,) = call(
        touch_kernel,
        [shape(8, LANES)],
        [factors],
        cost=pl.CostEstimate(flops=0, bytes_accessed=9 << 20, transcendentals=0),
    )
    (part,) = call(functools.partial(begin_kernel, sizes), [shape(cases, lanes)], [rhs, modes, fmap, *packs, touched])
    perm, back, lift, sums, start, solve, pairs = call(
        functools.partial(setup_kernel, sizes),
        [
            shape(6, dofs, dofs, dtype=bf16),
            shape(6, dofs, dofs, dtype=bf16),
            shape(12, 2 * LANES, dofs, dtype=bf16),
            shape(12, dofs, 2 * lanes, dtype=bf16),
            faces,
            shape(2 * LANES, 256 * slabs, dtype=bf16),
            shape(12, 32, dofs, dtype=bf16),
        ],
        [rhs, modes, fmap, coarse_rows, *packs],
        scratch=(pltpu.VMEM((LANES, dofs), f32), pltpu.VMEM((LANES, 256 * slabs), f32)),
        cost=pl.CostEstimate(flops=0, bytes_accessed=9 << 20, transcendentals=0),
    )

    def reduce(part, za, zb, along_y, along_x, also=None, image=None):
        za, zb, others = exchange(za, zb, "gz", part)
        outs = [shape(cases, face.shape[1] + lanes) for face in along_y] + [shape(cases, lanes)]
        ins = [part, *others, *along_y]
        *along_y, part = call(functools.partial(column_kernel, 1 + len(others)), outs, ins)
        ya, yb, others = exchange(*(along_y or (part, part)), "gy", part)
        outs = [shape(cases, face.shape[1] + whole) for face in along_x] + [shape(cases, whole)]
        if also is not None:
            part, also = lax.optimization_barrier((part, also))
        ins = [part, *others, *place, *along_x]
        *along_x, part = call(functools.partial(place_kernel, sizes, nc, 1 + len(others)), outs, ins)
        early = None
        if image is not None:
            (early,) = call(
                functools.partial(early_kernel, sizes),
                [faces],
                [pattern, turned, perm, image, ya, yb, za, zb],
                specs={0: smem},
                cost=pl.CostEstimate(flops=0, bytes_accessed=7 << 20, transcendentals=0),
            )
        xa, xb, others = exchange(*(along_x or (part, part)), "gx", part)
        return [xa, xb, ya, yb, za, zb], [part, *others], also, early

    _, parts, turned, _ = reduce(part, part, part, (), (), turned)
    wide = shape(cases, 2 * dofs)
    sends = [wide] * 4 + [shape(cases, dofs + lanes)] * 2 + [shape(cases, lanes)]
    residual, forward, image, *out = call(
        functools.partial(first_kernel, sizes, len(parts)),
        [faces, faces, faces] + sends,
        [pattern, factors, turned, perm, back, lift, sums, solve, start, *parts],
        specs={0: smem},
    )
    old = []
    for iteration in range(ITERS - 1):
        xa, xb, ya, yb, za, zb, part = out
        if iteration == 0:
            (lifted,) = call(
                functools.partial(lifted_kernel, sizes),
                [shape(12, 2 * LANES, dofs, dtype=bf16)],
                [pattern, turned, perm, pairs],
                specs={0: smem},
                scratch=(pltpu.VMEM((12, LANES, dofs), f32),),
                cost=pl.CostEstimate(flops=0, bytes_accessed=9 << 20, transcendentals=0),
            )
            got, parts, lifted, early = reduce(part, za, zb, (ya, yb), (xa, xb), lifted, image)
        else:
            got, parts, _, early = reduce(part, za, zb, (ya, yb), (xa, xb), None, image)
        residual, forward, image, *out = call(
            functools.partial(middle_kernel, sizes, nc, iteration == 0, len(parts)),
            [faces] * 6 + [shape(2, 3, cases, dofs), shape(8, LANES), faces] + sends,
            [pattern, factors, turned, perm, back, lift, sums, solve, lifted, early, *got, *parts, residual, forward, image, *old],
            specs={0: smem},
        )
        old, out = out[:6], out[6:]
    xa, xb, ya, yb, za, zb, part = out
    got, parts, _, _ = reduce(part, za, zb, (ya, yb), (xa, xb))
    multipliers, final = call(
        functools.partial(last_kernel, sizes, nc, len(parts)),
        [shape(2, 3, cases, dofs)] * 2,
        [lift, solve, *got, *parts, residual, forward, image, *old[:5]],
    )
    return multipliers.reshape(dual_rhs.shape), final.reshape(dual_rhs.shape)


def solution(mesh):
    return jax.shard_map(
        per_device,
        mesh=mesh,
        in_specs=(
            P("gx", "gy", "gz", None, None, None),
            P("gx", "gy", "gz", None, None, None, None),
            P("gx", "gy", "gz", None, None),
            P("gx", "gy", "gz", None, None),
            P("gx", "gy", "gz", None, None, None),
            P(("gx", "gy", "gz"), None),
        ),
        out_specs=(P("gx", "gy", "gz", None, None, None), P("gx", "gy", "gz", None, None, None)),
        check_vma=False,
    )
```

```python
import functools

import jax
import jax.numpy as jnp
from jax import lax
from jax.experimental import pallas as pl
from jax.experimental.pallas import tpu as pltpu
from jax.sharding import PartitionSpec as P

ITERS = 4
AXES = ("gx", "gy", "gz")
LANES = 128
SLOT = 8
SLOTS = 12
SCALARS = 3
NT = (((1,), (1,)), ((), ()))
NN = (((1,), (0,)), ((), ()))
TN = (((0,), (0,)), ((), ()))
f32 = jnp.float32
bf16 = jnp.bfloat16


def own_slot(s):
    return s


COLUMN_OF_FACE = {0: 2, 3: 1, 1: 4, 4: 3}


def whole_lanes(nc):
    return -(-(nc + SCALARS) // 256) * 256


def column_lanes(levels):
    return -(-(30 * levels + SCALARS) // LANES) * LANES


def nbr_slot(s, f):
    if f == 0:
        return 4 + s
    if f == 3:
        return 2 + s
    if f == 1:
        return 8 + s
    if f == 4:
        return 6 + s
    if f == 2:
        return 1 if s == 0 else 11
    return 10 if s == 0 else 0


def split2(x):
    high = x.astype(bf16)
    low = (x - high.astype(f32)).astype(bf16)
    return jnp.concatenate([high, low], 0)


def split3(x):
    high = x.astype(bf16)
    rest = x - high.astype(f32)
    mid = rest.astype(bf16)
    low = (rest - mid.astype(f32)).astype(bf16)
    return jnp.concatenate([high, mid, low], 0)


def fold2(x):
    n = x.shape[0] // 2
    return x[:n] + x[n:]


def fold3(x):
    n = x.shape[0] // 3
    return x[:n] + (x[n : 2 * n] + x[2 * n :])


def mm(a, b, dims):
    return lax.dot_general(a, b, dims, preferred_element_type=f32)


def position(sizes):
    index = [lax.axis_index(a) for a in AXES]
    parity = [lax.rem(i, 2) == 1 for i in index]
    masks = []
    for s in range(2):
        row = []
        for f in range(6):
            d = f % 3
            if d == 2 and (s == 0) == (f == 2):
                row.append(None)
            else:
                inside = (index[d] < sizes[d] - 1) if f < 3 else (index[d] > 0)
                row.append(inside.astype(f32))
        masks.append(row)
    return parity, masks


def masked(value, mask):
    return value if mask is None else value * mask


def pick(cond, a, b):
    return jnp.where(cond, a, b)


def pack_kernel(rhs_in, modes_in, fmap_in, coarse_in, rhs, modes, fmap, coarse, xa, xb, ya, yb, za, zb, sems):
    parity, _ = position((1, 1, 1))
    loads = ((rhs_in, rhs), (modes_in, modes), (fmap_in, fmap), (coarse_in, coarse))
    copies = [pltpu.make_async_copy(source, target, sems.at[k]) for k, (source, target) in enumerate(loads)]
    for copy in copies:
        copy.start()
    for copy in copies:
        copy.wait()
    slabs = -(-coarse.shape[1] // 256)
    for d, outs in ((0, (xa, xb)), (1, (ya, yb))):
        for s in range(2):
            up, down = modes[d, :, s, :], modes[d + 3, :, s, :]
            first = pick(parity[d], down, up)
            second = pick(parity[d], up, down)
            for out, piece in zip(outs, (first, second)):
                out[24 * s : 24 * s + 16, :] = rhs[s, d]
                out[24 * s + 16 : 24 * s + 24, :] = jnp.concatenate(
                    [piece, fmap[d, s : s + 1, :].astype(f32), jnp.zeros((1, 256), f32)], 0
                )
    up, down = modes[2, :, 1, :], modes[5, :, 0, :]
    for out, piece in zip((za, zb), (pick(parity[2], down, up), pick(parity[2], up, down))):
        out[0:16, :] = rhs[1, 2]
        out[16:24, :] = jnp.concatenate([piece, fmap[2, 1:2, :].astype(f32), jnp.zeros((1, 256), f32)], 0)
    for k in range(slabs):
        width = min(256, coarse.shape[1] - 256 * k)
        slab = coarse[:, 256 * k : 256 * k + width]
        if width < 256:
            slab = jnp.concatenate([slab, jnp.zeros((12, 256 - width), f32)], 1)
        gap = jnp.zeros((2, 256), f32)
        slab = jnp.concatenate([slab[:6], gap, slab[6:], gap], 0)
        for out, base in ((xa, 48), (xb, 48), (ya, 48), (yb, 48), (za, 24), (zb, 24)):
            out[base + 16 * k : base + 16 * k + 16, :] = slab


def sides_of(parity, packs):
    plus, minus = [], []
    for d in range(3):
        va, vb = packs[2 * d][...], packs[2 * d + 1][...]
        plus.append(pick(parity[d], vb, va))
        minus.append(pick(parity[d], va, vb))
    return plus, minus


def onehot(row):
    line = lax.broadcasted_iota(jnp.int32, (256, 256), 0)
    return (line == row.astype(jnp.int32)).astype(bf16)


def lower_map(fmap, minus, s, d):
    if d == 2 and s == 1:
        return fmap[2, 0:1, :]
    base = 24 * s if d < 2 else 0
    return minus[d][base + 22 : base + 23, :]


def lower_values(rhs, minus, s, d):
    if d == 2 and s == 1:
        return rhs[0, 2]
    base = 24 * s if d < 2 else 0
    inside = lax.axis_index(AXES[d]) > 0
    return minus[d][base : base + 16, :] * inside.astype(f32)


def begin_kernel(sizes, rhs, modes, fmap, xa, xb, ya, yb, za, zb, part):
    parity, _ = position((1, 1, 1))
    levels = 2 * sizes[2]
    lanes = part.shape[1]
    _, minus = sides_of(parity, (xa, xb, ya, yb, za, zb))
    zero2 = jnp.zeros((2, 256), f32)
    total = jnp.zeros((16, lanes), f32)
    for s in range(2):
        sums = jnp.zeros((48, 16), f32)
        for f in range(6):
            d = f % 3
            if f < 3:
                left = split3(rhs[s, f])
            else:
                table_rows = onehot(lower_map(fmap, minus, s, d))
                left = -mm(split3(lower_values(rhs, minus, s, d)), table_rows, NN)
                left = left.astype(bf16)
            sums += mm(left, split2(jnp.concatenate([modes[f, :, s, :], zero2], 0)), NT)
        own = fold3(sums)
        own = own[:, :8] + own[:, 8:]
        mode = lax.broadcasted_iota(jnp.int32, (8, lanes), 0)
        lane = lax.broadcasted_iota(jnp.int32, (8, lanes), 1)
        level = 2 * lax.axis_index("gz") + s
        choose = ((lane == level * 6 + mode) & (mode < 6)).astype(bf16)
        total += fold3(mm(split3(own), choose, NN))
    part[...] = total


def place_rows(sizes, nc, lanes, width, k):
    gx, gy = lax.axis_index("gx"), lax.axis_index("gy")
    levels = 2 * sizes[2]
    line = lax.broadcasted_iota(jnp.int32, (lanes, 1), 0)
    whole = lax.broadcasted_iota(jnp.int32, (lanes, width), 1)
    y = jnp.bitwise_xor(gy, k)
    aim = jnp.where(line >= 30 * levels, nc + line - 30 * levels, -1)
    for t, (dx, dy) in enumerate(((0, 0), (-1, 0), (1, 0), (0, -1), (0, 1))):
        inside = (gx + dx >= 0) & (gx + dx < sizes[0]) & (y + dy >= 0) & (y + dy < sizes[1])
        first = jnp.where(inside, ((gx + dx) * sizes[1] + y + dy - t) * 6 * levels, -6 * nc)
        aim = jnp.where((line >= t * 6 * levels) & (line < (t + 1) * 6 * levels), line + first, aim)
    return (whole == aim).astype(bf16)


def place_table_kernel(sizes, nc, lanes, place):
    for k in range(sizes[1]):
        place[k * lanes : k * lanes + lanes, :] = place_rows(sizes, nc, lanes, place.shape[1], k)


def touch_kernel(factors, out):
    out[...] = factors[0, 0, 0, 0:16, 0:LANES].astype(f32)[:8]


def turn_kernel(factors, touched, turned):
    for s in range(factors.shape[0]):
        for i in range(factors.shape[1]):
            for j in range(factors.shape[2]):
                turned[s, i, j] = factors[s, i, j].T


def setup_kernel(sizes, rhs, modes, fmap, coarse, xa, xb, ya, yb, za, zb, *refs):
    perm, back, lift, sums, start, solve, pairs, work, rows = refs
    parity, _ = position((1, 1, 1))
    nc = coarse.shape[1]
    slabs = -(-nc // 256)
    levels = 2 * sizes[2]
    lanes = column_lanes(levels)
    gz = lax.axis_index("gz")
    plus, minus = sides_of(parity, (xa, xb, ya, yb, za, zb))

    def to_upper_order(values, table_rows):
        return -fold3(mm(split3(values), table_rows, NT))

    zero2 = jnp.zeros((2, 256), f32)
    lane_column = lax.broadcasted_iota(jnp.int32, (16, lanes), 1)
    source_row = lax.broadcasted_iota(jnp.int32, (16, lanes), 0)
    tilde_low = {}
    for s in range(2):
        for d in range(3):
            table_rows = onehot(lower_map(fmap, minus, s, d))
            perm[s * 3 + d] = table_rows
            back[s * 3 + d] = table_rows.T
            tilde_low[s, d] = to_upper_order(modes[d + 3, :, s, :], table_rows)
    work[...] = jnp.zeros(work.shape, f32)
    for s in range(2):
        for f in range(6):
            d = f % 3
            base = 24 * s if d < 2 else 0
            if f < 3:
                own = modes[f, :, s, :]
                start[s, f] = rhs[s, f]
                if d == 2 and s == 0:
                    other = tilde_low[1, 2]
                else:
                    other = to_upper_order(plus[d][base + 16 : base + 22, :], onehot(fmap[d, s : s + 1, :]))
            else:
                own = tilde_low[s, d]
                start[s, f] = lower_values(rhs, minus, s, d)
                other = modes[2, :, 0, :] if d == 2 and s == 1 else minus[d][base + 16 : base + 22, :]
            own = jnp.concatenate([own, zero2], 0)
            other = jnp.concatenate([other, zero2], 0)
            at, n = own_slot(s) * SLOT, nbr_slot(s, f) * SLOT
            work[at : at + 8, :] = own
            work[n : n + 8, :] = other
            lift[s * 6 + f] = split2(work[...])
            work[at : at + 8, :] = jnp.zeros((8, 256), f32)
            work[n : n + 8, :] = jnp.zeros((8, 256), f32)
            pair = split2(jnp.concatenate([own, other], 0))
            pairs[s * 6 + f] = pair
            level = 2 * gz + s
            if d == 2:
                target = (level + (1 if f == 2 else -1)) * 6
            else:
                target = COLUMN_OF_FACE[f] * 6 * levels + level * 6
            mode = jnp.bitwise_and(source_row, 7)
            aim = jnp.where(source_row < 8, level * 6, target) + mode
            both = ((lane_column == aim) & (mode < 6)).astype(bf16)
            for h in range(2):
                half = pair[16 * h : 16 * h + 16]
                sums[s * 6 + f, :, h * lanes : h * lanes + lanes] = mm(half, both, TN).astype(bf16)

    rows[...] = jnp.zeros(rows.shape, f32)
    pieces = [(2, minus[0], 48, 16), (4, plus[0], 48, 16), (6, minus[1], 48, 16), (8, plus[1], 48, 16)]
    pieces += [(10, minus[2], 24 + 8, 8), (11, plus[2], 24, 8)]
    for k in range(slabs):
        width = min(256, nc - 256 * k)
        slab = coarse[:, 256 * k : 256 * k + width]
        if width < 256:
            slab = jnp.concatenate([slab, jnp.zeros((12, 256 - width), f32)], 1)
        slab = jnp.concatenate([slab[:6], zero2, slab[6:], zero2], 0)
        rows[0:16, 256 * k : 256 * k + 256] = slab
        for slot, source, base, count in pieces:
            rows[slot * SLOT : slot * SLOT + count, 256 * k : 256 * k + 256] = source[
                base + 16 * k : base + 16 * k + count, :
            ]
    solve[...] = split2(rows[...])


def tail(ref, lanes):
    return ref[:, ref.shape[1] - lanes :]


def beside(outs, faces, values):
    if faces:
        for out, face in zip(outs, faces):
            width = face.shape[1]
            out[:, :width] = face[...]
            out[:, width:] = values
    outs[-1][...] = values


def column_kernel(count, *refs):
    lanes = refs[0].shape[1]
    total = refs[0][...]
    for part in refs[1:count]:
        total += tail(part, lanes)
    split = count + (len(refs) - count) // 2
    beside(refs[split:], refs[count:split], total)


def place_kernel(sizes, nc, count, *refs):
    lanes, width = refs[0].shape[1], refs[-1].shape[1]
    lefts = [split3(tail(part, lanes)) for part in refs[:count]]
    faces = (len(refs) - count) // 2
    if (len(refs) - count) % 2:
        total = jnp.zeros((lefts[0].shape[0], width), f32)
        for k, left in enumerate(lefts):
            total += mm(left, place_rows(sizes, nc, lanes, width, k), NN)
        split = count + faces
    else:
        total = mm(jnp.concatenate(lefts, 1), refs[count][...], NN)
        count, split = count + 1, count + faces
    beside(refs[split:], refs[count:split], fold3(total))


def coarse(whole, parts, solve):
    total = whole[...]
    for part in parts:
        total += tail(part, whole.shape[1])
    got = fold3(mm(split3(total[:, : solve.shape[1]]), solve[...], NT))
    return total, got[:, :LANES] + got[:, LANES:]


def lift_left(total):
    left = split3(total)
    return jnp.concatenate([left, left], 1)


def forward_faces(faces, js, pattern, turned, perm):
    sums = {}
    for s in range(2):
        sides = {}
        for j in js:
            rows = faces[s, j]
            sides[j] = rows if j < 3 else (-mm(rows, perm[s * 3 + j - 3], NN)).astype(bf16)
        for i in range(6):
            acc = jnp.zeros((32, 256), f32)
            for j in js:
                acc += mm(sides[j] * pattern[i, s, j].astype(f32).astype(bf16), turned[s, i, j], NN)
            sums[s, i] = acc
    return sums


def lifted_kernel(sizes, pattern, turned, perm, pairs, out, work):
    _, masks = position(sizes)
    for s in range(2):
        for i in range(6):
            work[s * 6 + i] = jnp.zeros((LANES, 256), f32)
    for j in range(6):
        faces = {}
        for s in range(2):
            rows = pairs[s * 6 + j]
            faces[s, j] = rows if masks[s][j] is None else (rows.astype(f32) * masks[s][j]).astype(bf16)
        sums = forward_faces(faces, (j,), pattern, turned, perm)
        for s in range(2):
            at, n = own_slot(s) * SLOT, nbr_slot(s, j) * SLOT
            for i in range(6):
                got = fold2(sums[s, i])
                work[s * 6 + i, at : at + 8, :] += got[:8]
                work[s * 6 + i, n : n + 8, :] += got[8:]
    for k in range(12):
        out[k] = split2(work[k])


def sum_of_sides(s, f, image, pair, parity, mask):
    d = f % 3
    if pair is None:
        other = image[1 - s, 5 if f == 2 else 2]
    else:
        at = 256 * s if d < 2 else 0
        va, vb = (face[:, at : at + 256] for face in pair)
        other = pick(parity[d], vb, va) if f < 3 else pick(parity[d], va, vb)
    return masked(image[s, f] + other, mask)


def early_kernel(sizes, pattern, turned, perm, image, ya, yb, za, zb, out):
    parity, masks = position(sizes)
    faces = {}
    for s in range(2):
        for f in (1, 2, 4, 5):
            inner = f % 3 == 2 and (s == 0) == (f == 2)
            pair = None if inner else (ya, yb) if f % 3 == 1 else (za, zb)
            faces[s, f] = split2(sum_of_sides(s, f, image, pair, parity, masks[s][f]))
    sums = forward_faces(faces, (1, 2, 4, 5), pattern, turned, perm)
    for s in range(2):
        for i in range(6):
            out[s, i] = fold2(sums[s, i])


def apply_factors(residual, pattern, factors, turned, perm, back, sums, masks, parity, previous, forward, image, sends, given=None):
    xa, xb, ya, yb, za, zb, part = sends
    lanes = part.shape[1]
    partial = jnp.zeros((48, 2 * lanes), f32)
    own_sum = jnp.zeros((16, 256), f32)
    square = jnp.zeros((16, 256), f32)
    cross = jnp.zeros((16, 256), f32)
    faces = {}
    for s in range(2):
        sides = []
        for j in range(6):
            value = residual[s][j]
            if j < 3:
                own_sum += value * value
                sides.append(split2(value))
            elif given is None:
                sides.append((-mm(split2(value), perm[s * 3 + j - 3], NN)).astype(bf16))
        present = [[pattern[i, s, j].astype(f32).astype(bf16) for j in range(6)] for i in range(6)]
        halves = []
        for i in range(6):
            if given is None:
                acc = jnp.zeros((32, 256), f32)
                for j in range(6):
                    acc += mm(sides[j] * present[i][j], turned[s, i, j], NN)
                got = fold2(acc)
            else:
                got = given[s, i]
            forward[s, i] = got
            square += got * got
            if previous is not None:
                cross += got * previous[s][i]
            halves.append(split2(got))
        for j in range(6):
            acc = jnp.zeros((32, 256), f32)
            for i in range(6):
                acc += mm(halves[i] * present[i][j], factors[s, i, j], NN)
            got = fold2(acc)
            if j >= 3:
                got = -fold3(mm(split3(got), back[s * 3 + j - 3], NN))
            got = masked(got, masks[s][j])
            image[s, j] = got
            faces[s, j] = got
            partial += mm(split3(got), sums[s * 6 + j], NN)
    for s in range(2):
        at = slice(256 * s, 256 * s + 256)
        xa[:, at] = pick(parity[0], faces[s, 3], faces[s, 0])
        xb[:, at] = pick(parity[0], faces[s, 0], faces[s, 3])
        ya[:, at] = pick(parity[1], faces[s, 4], faces[s, 1])
        yb[:, at] = pick(parity[1], faces[s, 1], faces[s, 4])
    total = fold3(partial)
    total = total[:, :lanes] + total[:, lanes:]
    lane = lax.broadcasted_iota(jnp.int32, total.shape, 1)
    scalars = 30 * 2 * lax.axis_size("gz")
    for k, values in enumerate((own_sum, square, cross)):
        total = jnp.where(lane == scalars + k, jnp.sum(values, axis=1, keepdims=True), total)
    part[...] = total
    for out, face in ((za, pick(parity[2], faces[0, 5], faces[1, 2])), (zb, pick(parity[2], faces[1, 2], faces[0, 5]))):
        out[:, :256] = face
        out[:, 256:] = total


def first_kernel(sizes, count, pattern, factors, turned, perm, back, lift, sums, solve, start, *refs):
    parity, masks = position(sizes)
    residual, forward, image = refs[count : count + 3]
    left = lift_left(coarse(refs[0], refs[1:count], solve)[1])
    now = [[None] * 6 for _ in range(2)]
    for s in range(2):
        for f in range(6):
            value = start[s, f] - masked(fold3(mm(left, lift[s * 6 + f], NN)), masks[s][f])
            residual[s, f] = value
            now[s][f] = value
    apply_factors(now, pattern, factors, turned, perm, back, sums, masks, parity, None, forward, image, refs[count + 3 :])


def update(sizes, nc, first, faces, parts, state, count):
    parity, masks = position(sizes)
    residual, forward, image, lift, solve, old = state
    total, solution_part = coarse(parts[0], parts[1:], solve)
    left = lift_left(solution_part)
    sums = jnp.sum(total, axis=0, keepdims=True)
    lane = lax.broadcasted_iota(jnp.int32, sums.shape, 1)

    def scalar(k):
        return jnp.sum(jnp.where(lane == nc + k, sums, 0.0), axis=1, keepdims=True)

    rho, curvature = scalar(0), scalar(1)
    if first:
        beta = None
    else:
        direction, moved, along, multipliers, scalars = old[:5]
        beta = rho / scalars[0:1, 0:1]
        curvature = curvature + 2.0 * beta * scalar(2) + beta * beta * scalars[1:2, 0:1]
    step = rho / curvature
    out, jumps = {}, {}
    for s in range(2):
        for f in range(count):
            d = f % 3
            inner = d == 2 and (s == 0) == (f == 2)
            pair = None if inner else faces[2 * d : 2 * d + 2]
            change = sum_of_sides(s, f, image, pair, parity, masks[s][f])
            if d == 0:
                jumps[s, f] = split2(change)
            change -= masked(fold3(mm(left, lift[s * 6 + f], NN)), masks[s][f])
            value = residual[s, f]
            towards = value
            if not first:
                towards = value + beta * direction[s, f]
                change = change + beta * moved[s, f]
            out[s, f] = (value - step * change, towards, change)
            if f < 3:
                gain = step * towards
                out[s, f] += (gain if first else multipliers[s, f] + gain,)
    return parity, masks, beta, rho, curvature, out, left, step, jumps


def middle_kernel(sizes, nc, first, count, *refs):
    pattern, factors, turned, perm, back, lift, sums, solve, lifted, early = refs[:10]
    faces, parts = refs[10:16], refs[16 : 16 + count]
    residual, forward, image = refs[16 + count : 19 + count]
    rest = refs[19 + count :]
    if first:
        old = None
    else:
        old, rest = rest[:6], rest[6:]
    new_residual, new_forward, new_image, new_direction, new_moved, new_along, new_multipliers, new_scalars = rest[:8]
    new_pushed = rest[8]
    parity, masks, beta, rho, curvature, out, left, step, jumps = update(
        sizes, nc, first, faces, parts, (residual, forward, image, lift, solve, old), 6
    )
    sides = forward_faces(jumps, (0, 3), pattern, turned, perm)
    given = {}
    for s in range(2):
        for i in range(6):
            pushed = early[s, i] + fold2(sides[s, i]) - fold3(mm(left, lifted[s * 6 + i], NN))
            if not first:
                pushed += beta * old[5][s, i]
            new_pushed[s, i] = pushed
            given[s, i] = forward[s, i] - step * pushed
    row = lax.broadcasted_iota(jnp.int32, (8, LANES), 0)
    new_scalars[...] = jnp.where(row == 0, rho, curvature)
    now = [[None] * 6 for _ in range(2)]
    along = [[None] * 6 for _ in range(2)]
    for s in range(2):
        for f in range(6):
            values = out[s, f]
            now[s][f] = values[0]
            new_residual[s, f] = values[0]
            new_direction[s, f] = values[1]
            new_moved[s, f] = values[2]
            if f < 3:
                new_multipliers[s, f] = values[3]
            line = forward[s, f] if first else forward[s, f] + beta * old[2][s, f]
            along[s][f] = line
            new_along[s, f] = line
    apply_factors(now, pattern, factors, turned, perm, back, sums, masks, parity, along, new_forward, new_image, rest[9:], given)


def last_kernel(sizes, nc, count, lift, solve, *refs):
    faces, parts = refs[:6], refs[6 : 6 + count]
    residual, forward, image = refs[6 + count : 9 + count]
    old = refs[9 + count : 14 + count]
    multipliers, final = refs[14 + count :]
    out = update(sizes, nc, False, faces, parts, (residual, forward, image, lift, solve, old), 3)[5]
    for s in range(2):
        for f in range(3):
            final[s, f] = out[s, f][0]
            multipliers[s, f] = out[s, f][3]


def swap(values, axis, distance):
    return lax.ppermute(values, axis, [(i, i ^ distance) for i in range(lax.axis_size(axis))])


def exchange(first, second, axis, alone=None, ends=True):
    size = lax.axis_size(axis)
    below = swap(first, axis, 1)
    if size == 2:
        return below, below, [below]
    pairs = [(i, i + 1 if i % 2 else i - 1) for i in range(size)]
    if ends:
        pairs = [(i, j % size) for i, j in pairs]
    else:
        pairs = [(i, j) for i, j in pairs if 0 <= j < size]
    above = lax.ppermute(second, axis, pairs)
    others = [below]
    if alone is not None:
        for distance in range(2, size):
            others.append(above if size == 4 and distance == 3 else swap(alone, axis, distance))
    return below, above, others


def per_device(dual_rhs, factors, block_pattern, face_map, rigid_modes, coarse_solve):
    sizes = tuple(lax.axis_size(a) for a in AXES)
    cases, dofs = dual_rhs.shape[4:]
    nc = coarse_solve.shape[1]
    slabs = -(-nc // 256)
    rhs = dual_rhs.reshape(dual_rhs.shape[2:])
    factors = factors.reshape(factors.shape[2:])
    pattern = block_pattern.reshape(block_pattern.shape[2:]).transpose(1, 0, 2)
    fmap = face_map.reshape(face_map.shape[2:]).transpose(1, 0, 2)
    modes = rigid_modes.reshape(rigid_modes.shape[2:]).transpose(1, 2, 0, 3)
    vmem = pl.BlockSpec(memory_space=pltpu.VMEM)
    smem = pl.BlockSpec(memory_space=pltpu.SMEM)
    params = pltpu.CompilerParams(vmem_limit_bytes=24 << 20)

    def shape(*dims, dtype=f32):
        return jax.ShapeDtypeStruct(dims, dtype)

    anywhere = pl.BlockSpec(memory_space=pl.ANY)

    def call(kernel, outs, ins, specs=None, scratch=(), cost=None):
        specs = specs or {}
        return pl.pallas_call(
            kernel,
            out_shape=outs,
            in_specs=[specs.get(i, vmem) for i in range(len(ins))],
            out_specs=[vmem] * len(outs),
            scratch_shapes=list(scratch),
            compiler_params=params,
            cost_estimate=cost,
        )(*ins)

    levels = 2 * sizes[2]
    lanes, whole = column_lanes(levels), whole_lanes(nc)
    packs = [shape(48 + 16 * slabs, dofs)] * 4 + [shape(24 + 16 * slabs, dofs)] * 2
    raw = [rhs, modes, fmap, coarse_solve]
    rhs, modes, fmap, coarse_rows, xa, xb, ya, yb, za, zb = call(
        pack_kernel,
        [jax.ShapeDtypeStruct(x.shape, x.dtype) for x in raw] + packs,
        raw,
        specs={i: anywhere for i in range(4)},
        scratch=(pltpu.SemaphoreType.DMA((4,)),),
    )
    place = []
    if sizes[1] * lanes * whole <= 1 << 20:
        place = call(
            functools.partial(place_table_kernel, sizes, nc, lanes),
            [shape(sizes[1] * lanes, whole, dtype=bf16)],
            [],
            cost=pl.CostEstimate(flops=0, bytes_accessed=4 << 20, transcendentals=0),
        )
    za, zb, _ = exchange(za, zb, "gz", ends=False)
    xa, xb, _ = exchange(xa, xb, "gx", ends=False)
    ya, yb, _ = exchange(ya, yb, "gy", ends=False)
    packs = [xa, xb, ya, yb, za, zb]
    faces = shape(2, 6, cases, dofs)
    (touched,) = call(
        touch_kernel,
        [shape(8, LANES)],
        [factors],
        cost=pl.CostEstimate(flops=0, bytes_accessed=9 << 20, transcendentals=0),
    )
    (part,) = call(functools.partial(begin_kernel, sizes), [shape(cases, lanes)], [rhs, modes, fmap, *packs])
    perm, back, lift, sums, start, solve, pairs = call(
        functools.partial(setup_kernel, sizes),
        [
            shape(6, dofs, dofs, dtype=bf16),
            shape(6, dofs, dofs, dtype=bf16),
            shape(12, 2 * LANES, dofs, dtype=bf16),
            shape(12, dofs, 2 * lanes, dtype=bf16),
            faces,
            shape(2 * LANES, 256 * slabs, dtype=bf16),
            shape(12, 32, dofs, dtype=bf16),
        ],
        [rhs, modes, fmap, coarse_rows, *packs],
        scratch=(pltpu.VMEM((LANES, dofs), f32), pltpu.VMEM((LANES, 256 * slabs), f32)),
        cost=pl.CostEstimate(flops=0, bytes_accessed=9 << 20, transcendentals=0),
    )

    def reduce(part, za, zb, along_y, along_x, also=None, image=None):
        za, zb, others = exchange(za, zb, "gz", part)
        outs = [shape(cases, face.shape[1] + lanes) for face in along_y] + [shape(cases, lanes)]
        ins = [part, *others, *along_y]
        *along_y, part = call(functools.partial(column_kernel, 1 + len(others)), outs, ins)
        ya, yb, others = exchange(*(along_y or (part, part)), "gy", part)
        outs = [shape(cases, face.shape[1] + whole) for face in along_x] + [shape(cases, whole)]
        if also is not None:
            part, also = lax.optimization_barrier((part, also))
        ins = [part, *others, *place, *along_x]
        *along_x, part = call(functools.partial(place_kernel, sizes, nc, 1 + len(others)), outs, ins)
        early = None
        if image is not None:
            (early,) = call(
                functools.partial(early_kernel, sizes),
                [faces],
                [pattern, turned, perm, image, ya, yb, za, zb],
                specs={0: smem},
                cost=pl.CostEstimate(flops=0, bytes_accessed=7 << 20, transcendentals=0),
            )
        xa, xb, others = exchange(*(along_x or (part, part)), "gx", part)
        return [xa, xb, ya, yb, za, zb], [part, *others], also, early

    _, parts, touched, _ = reduce(part, part, part, (), (), touched)
    (turned,) = call(
        turn_kernel,
        [jax.ShapeDtypeStruct(factors.shape, factors.dtype)],
        [factors, touched],
        cost=pl.CostEstimate(flops=0, bytes_accessed=9 << 20, transcendentals=0),
    )
    wide = shape(cases, 2 * dofs)
    sends = [wide] * 4 + [shape(cases, dofs + lanes)] * 2 + [shape(cases, lanes)]
    residual, forward, image, *out = call(
        functools.partial(first_kernel, sizes, len(parts)),
        [faces, faces, faces] + sends,
        [pattern, factors, turned, perm, back, lift, sums, solve, start, *parts],
        specs={0: smem},
    )
    old = []
    for iteration in range(ITERS - 1):
        xa, xb, ya, yb, za, zb, part = out
        if iteration == 0:
            (lifted,) = call(
                functools.partial(lifted_kernel, sizes),
                [shape(12, 2 * LANES, dofs, dtype=bf16)],
                [pattern, turned, perm, pairs],
                specs={0: smem},
                scratch=(pltpu.VMEM((12, LANES, dofs), f32),),
                cost=pl.CostEstimate(flops=0, bytes_accessed=9 << 20, transcendentals=0),
            )
            got, parts, lifted, early = reduce(part, za, zb, (ya, yb), (xa, xb), lifted, image)
        else:
            got, parts, _, early = reduce(part, za, zb, (ya, yb), (xa, xb), None, image)
        residual, forward, image, *out = call(
            functools.partial(middle_kernel, sizes, nc, iteration == 0, len(parts)),
            [faces] * 6 + [shape(2, 3, cases, dofs), shape(8, LANES), faces] + sends,
            [pattern, factors, turned, perm, back, lift, sums, solve, lifted, early, *got, *parts, residual, forward, image, *old],
            specs={0: smem},
        )
        old, out = out[:6], out[6:]
    xa, xb, ya, yb, za, zb, part = out
    got, parts, _, _ = reduce(part, za, zb, (ya, yb), (xa, xb))
    multipliers, final = call(
        functools.partial(last_kernel, sizes, nc, len(parts)),
        [shape(2, 3, cases, dofs)] * 2,
        [lift, solve, *got, *parts, residual, forward, image, *old[:5]],
    )
    return multipliers.reshape(dual_rhs.shape), final.reshape(dual_rhs.shape)


def solution(mesh):
    return jax.shard_map(
        per_device,
        mesh=mesh,
        in_specs=(
            P("gx", "gy", "gz", None, None, None),
            P("gx", "gy", "gz", None, None, None, None),
            P("gx", "gy", "gz", None, None),
            P("gx", "gy", "gz", None, None),
            P("gx", "gy", "gz", None, None, None),
            P(("gx", "gy", "gz"), None),
        ),
        out_specs=(P("gx", "gy", "gz", None, None, None), P("gx", "gy", "gz", None, None, None)),
        check_vma=False,
    )
```
